128 devices in a mesh: row: 8 (over x, z_lo), col: 16 (over y, z_hi, core).
Axes of the slice: x: 4, y: 4, z: 4 (z_hi: 2, z_lo: 2; z = z_hi * 2 + z_lo), core: 2. Of those that a mesh axis runs over, the one named last changes fastest.
Arguments:
- alignment_embedding: bfloat16 [64, 1536, 256], P('col', 'row'), may hold values from -6 to 6
- couplings_embedding: bfloat16 [1536, 1536, 128], P('row', 'col'), may hold values from -6 to 6
- alignment_availability: int32 [64, 1536], P('col', 'row'), may hold values 0 or 1
- amino_availability: int32 [1536], replicated, may hold values 0 or 1
- alignment_scaling_vector: float32 [256], replicated, may hold values from 0.3 to 3
- attention_joint_matrix: bfloat16 [256, 1024], replicated, may hold values from -0.375 to 0.375
- attention_final_matrix: bfloat16 [256, 256], replicated, may hold values from -0.375 to 0.375
- coupling_scaling_vector: float32 [128], replicated, may hold values from 0.3 to 3
- coupling_logit_matrix: bfloat16 [128, 8], replicated, may hold values from -8 to 8
- tensor_scaling_vector: float32 [256], replicated, may hold values from 0.3 to 3
- first_factor_matrix: bfloat16 [256, 32], replicated, may hold values from -0.375 to 0.375
- second_factor_matrix: bfloat16 [256, 32], replicated, may hold values from -0.375 to 0.375
- tensor_projection_matrix: bfloat16 [1024, 128], replicated, may hold values from -1.5 to 1.5
- tensor_offset_vector: float32 [128], replicated, may hold values from -3 to 3
Outputs:
- alignment_refreshed: bfloat16 [64, 1536, 256], P('col', 'row')
- couplings_refreshed: bfloat16 [1536, 1536, 128], P('row', 'col')
The draws below stay inside these ranges and needn't reach their ends.
All inputs are finite; a program needn't handle non-finite values. No bound on the sum of `alignment_availability` on one device may be relied on, other than what follows from the above.
Results may differ from the reference program's by a relative error of at most 0.027.
The reference program's roundings to bfloat16 on the way count: a program that leaves them out, or rounds other values in their place, can miss the bound.
Values may be sent and summed in bfloat16 or wider, within the bound.
No kernel may reach another device: no remote copies, remote signals or barrier semaphores. Data moves between devices by JAX's collectives and lax.ppermute only.
A program may use at most 128 MiB of HBM per device.

```python
import math
import jax
import jax.numpy as jnp
from jax import lax

ALIGNMENT_DEPTH = 256
H = 8
HEADWISE_DEPTH = 32
CZ = 128
PROJECTED_DEPTH = 32
ALIGNED_TOTAL = 64
AMINO_TOTAL = 1536


def draw_coupling_logit_matrix(key, part):
    key = jax.random.fold_in(key, 11)
    base = jax.random.normal(key, (CZ, H), jnp.float32)
    return (jnp.clip(base, -6.0, 6.0) * CZ ** (-0.5)).astype(jnp.bfloat16)


def touch_ends(drawn, own_key, least, top_value):
    longest = drawn.shape.index(max(drawn.shape))
    spots = []
    for shift in (0, 1):
        where = [jax.random.randint(jax.random.fold_in(own_key, axis), (), 0, length) for axis, length in enumerate(drawn.shape)]
        where[longest] = (where[longest] + shift) % drawn.shape[longest]
        spots.append(tuple(where))
    return drawn.at[spots[0]].set(least).at[spots[1]].set(top_value)


def level_of(stream_key, extent, cuts, smallest, high):
    level, own = 1.0, jax.random.fold_in(stream_key, 6)
    for position, parts in cuts:
        draws = jnp.exp(jax.random.uniform(jax.random.fold_in(own, position), (parts,), jnp.float32, smallest / len(cuts), high / len(cuts)))
        level = level * jnp.repeat(draws, extent[position] // parts).reshape([-1 if axis == position else 1 for axis in range(len(extent))])
    return level


def gaussian(own_key, extent, spread, bound, cuts=(), kind=jnp.bfloat16):
    values = jax.random.normal(own_key, extent, jnp.float32) * spread
    if len(cuts) > 0:
        values = level_of(own_key, extent, cuts, -0.22, 0.18) * values
    return jnp.clip(values, min=-bound, max=bound).astype(kind)


def setup_inputs(seed: int = 0) -> dict:
    arg_keys = jax.random.split(jax.random.key(seed), 15)
    alignment_embedding = gaussian(arg_keys[0], (ALIGNED_TOTAL, AMINO_TOTAL, ALIGNMENT_DEPTH), 1.0, 6.0, ((0, 16), (1, 8)))
    couplings_embedding = gaussian(arg_keys[1], (AMINO_TOTAL, AMINO_TOTAL, CZ), 1.0, 6.0, ((0, 8), (1, 16)))
    alignment_availability = touch_ends((jax.random.randint(arg_keys[2], (ALIGNED_TOTAL, AMINO_TOTAL), 0, 5) < 4).astype(jnp.int32), jax.random.fold_in(arg_keys[2], 1), 0, 1)
    amino_availability = touch_ends((jax.random.randint(arg_keys[3], (AMINO_TOTAL,), 0, 8) < 7).astype(jnp.int32), jax.random.fold_in(arg_keys[3], 1), 0, 1)
    alignment_scaling_vector = jnp.clip(jnp.exp(jax.random.uniform(arg_keys[4], (ALIGNMENT_DEPTH,), jnp.float32, math.log(0.3), math.log(3.0))), 0.3, 3.0)
    attention_joint_matrix = gaussian(arg_keys[5], (ALIGNMENT_DEPTH, 4 * ALIGNMENT_DEPTH), ALIGNMENT_DEPTH ** -0.5, 0.375)
    attention_final_matrix = gaussian(arg_keys[6], (ALIGNMENT_DEPTH, ALIGNMENT_DEPTH), ALIGNMENT_DEPTH ** -0.5, 0.375)
    coupling_scaling_vector = jnp.clip(jnp.exp(jax.random.uniform(arg_keys[7], (CZ,), jnp.float32, math.log(0.3), math.log(3.0))), 0.3, 3.0)
    coupling_logit_matrix = draw_coupling_logit_matrix(jax.random.fold_in(arg_keys[14], 71), 0)
    tensor_scaling_vector = jnp.clip(jnp.exp(jax.random.uniform(arg_keys[9], (ALIGNMENT_DEPTH,), jnp.float32, math.log(0.3), math.log(3.0))), 0.3, 3.0)
    first_factor_matrix = gaussian(arg_keys[10], (ALIGNMENT_DEPTH, PROJECTED_DEPTH), ALIGNMENT_DEPTH ** -0.5, 0.375)
    second_factor_matrix = gaussian(arg_keys[11], (ALIGNMENT_DEPTH, PROJECTED_DEPTH), ALIGNMENT_DEPTH ** -0.5, 0.375)
    tensor_projection_matrix = gaussian(arg_keys[12], (PROJECTED_DEPTH * PROJECTED_DEPTH, CZ), (max(1, PROJECTED_DEPTH * PROJECTED_DEPTH // ALIGNED_TOTAL)) ** -0.5, 1.5)
    tensor_offset_vector = gaussian(arg_keys[13], (CZ,), 0.5, 3.0, (), jnp.float32)
    return {"alignment_embedding": alignment_embedding, "couplings_embedding": couplings_embedding, "alignment_availability": alignment_availability, "amino_availability": amino_availability, "alignment_scaling_vector": alignment_scaling_vector, "attention_joint_matrix": attention_joint_matrix, "attention_final_matrix": attention_final_matrix, "coupling_scaling_vector": coupling_scaling_vector, "coupling_logit_matrix": coupling_logit_matrix, "tensor_scaling_vector": tensor_scaling_vector, "first_factor_matrix": first_factor_matrix, "second_factor_matrix": second_factor_matrix, "tensor_projection_matrix": tensor_projection_matrix, "tensor_offset_vector": tensor_offset_vector}


def standardize_lines(x, gain):
    x = x.astype(jnp.float32)
    mean = lax.optimization_barrier(jnp.mean(x, axis=-1, keepdims=True))
    var = lax.optimization_barrier(jnp.mean((x - mean) ** 2, axis=-1, keepdims=True))
    return (x - mean) * lax.rsqrt(var + 1e-05) * gain

def reference(alignment_embedding, couplings_embedding, alignment_availability, amino_availability, alignment_scaling_vector, attention_joint_matrix, attention_final_matrix, coupling_scaling_vector, coupling_logit_matrix, tensor_scaling_vector, first_factor_matrix, second_factor_matrix, tensor_projection_matrix, tensor_offset_vector):
    alignment_standardized = standardize_lines(alignment_embedding, alignment_scaling_vector).astype(jnp.bfloat16)
    joint_projected = jnp.dot(alignment_standardized.reshape(ALIGNED_TOTAL * AMINO_TOTAL, ALIGNMENT_DEPTH), attention_joint_matrix, preferred_element_type=jnp.float32).reshape(ALIGNED_TOTAL, AMINO_TOTAL, 4 * ALIGNMENT_DEPTH)
    asking_vectors = (joint_projected[:, :, :ALIGNMENT_DEPTH] * HEADWISE_DEPTH ** (-0.5)).astype(jnp.bfloat16)
    key = joint_projected[:, :, ALIGNMENT_DEPTH:2 * ALIGNMENT_DEPTH].astype(jnp.bfloat16)
    content_heads = joint_projected[:, :, 2 * ALIGNMENT_DEPTH:3 * ALIGNMENT_DEPTH].astype(jnp.bfloat16)
    sigmoid_switch = jax.nn.sigmoid(joint_projected[:, :, 3 * ALIGNMENT_DEPTH:])
    znorm = standardize_lines(couplings_embedding, coupling_scaling_vector).astype(jnp.bfloat16)
    bias = jnp.dot(znorm.reshape(AMINO_TOTAL * AMINO_TOTAL, CZ), coupling_logit_matrix, preferred_element_type=jnp.float32)
    bias = bias.reshape(AMINO_TOTAL, AMINO_TOTAL, H).astype(jnp.bfloat16).transpose(2, 0, 1).astype(jnp.float32)
    absent_logit_offset = (alignment_availability.astype(jnp.float32) - 1.0) * 1000000000.0

    def attend(items):
        q_seq, k_seq, content_vectors, m_seq = items
        q_seq = q_seq.reshape(AMINO_TOTAL, H, HEADWISE_DEPTH).astype(jnp.float32)
        k_seq = k_seq.reshape(AMINO_TOTAL, H, HEADWISE_DEPTH).astype(jnp.float32)
        content_vectors = content_vectors.reshape(AMINO_TOTAL, H, HEADWISE_DEPTH).astype(jnp.float32)
        scores = jnp.einsum('ihd,jhd->hij', q_seq, k_seq) + bias + m_seq[None, None, :]
        attention_probabilities = jax.nn.softmax(scores, axis=-1).astype(jnp.bfloat16).astype(jnp.float32)
        return jnp.einsum('ktc,cko->tko', attention_probabilities, content_vectors).reshape(AMINO_TOTAL, ALIGNMENT_DEPTH)
    attended = lax.map(attend, (asking_vectors, key, content_heads, absent_logit_offset))
    switched_attention = (sigmoid_switch * attended).astype(jnp.bfloat16)
    increment_tensor = jnp.dot(switched_attention.reshape(ALIGNED_TOTAL * AMINO_TOTAL, ALIGNMENT_DEPTH), attention_final_matrix, preferred_element_type=jnp.float32).reshape(ALIGNED_TOTAL, AMINO_TOTAL, ALIGNMENT_DEPTH)
    alignment_refreshed = (alignment_embedding.astype(jnp.float32) + increment_tensor).astype(jnp.bfloat16)
    tensor_standardized = standardize_lines(alignment_refreshed, tensor_scaling_vector).astype(jnp.bfloat16)
    availability_indicators = alignment_availability.astype(jnp.float32)[:, :, None]
    first_factor = (jnp.dot(tensor_standardized.reshape(ALIGNED_TOTAL * AMINO_TOTAL, ALIGNMENT_DEPTH), first_factor_matrix, preferred_element_type=jnp.float32).reshape(ALIGNED_TOTAL, AMINO_TOTAL, PROJECTED_DEPTH) * availability_indicators).astype(jnp.bfloat16)
    second_factor = (jnp.dot(tensor_standardized.reshape(ALIGNED_TOTAL * AMINO_TOTAL, ALIGNMENT_DEPTH), second_factor_matrix, preferred_element_type=jnp.float32).reshape(ALIGNED_TOTAL, AMINO_TOTAL, PROJECTED_DEPTH) * availability_indicators).astype(jnp.bfloat16)
    right_f = second_factor.astype(jnp.float32)

    def outer_rows(left_block):
        outer = jnp.einsum('sia,sjb->ijab', left_block.astype(jnp.float32), right_f) / ALIGNED_TOTAL
        outer = outer.astype(jnp.bfloat16).reshape(-1, PROJECTED_DEPTH * PROJECTED_DEPTH)
        return (jnp.dot(outer, tensor_projection_matrix, preferred_element_type=jnp.float32) + tensor_offset_vector).reshape(-1, AMINO_TOTAL, CZ)
    blocks = first_factor.reshape(ALIGNED_TOTAL, AMINO_TOTAL // 4, 4, PROJECTED_DEPTH).transpose(1, 0, 2, 3)
    pair_update = lax.map(outer_rows, blocks).reshape(AMINO_TOTAL, AMINO_TOTAL, CZ)
    keep = amino_availability.astype(jnp.float32)
    couplings_refreshed = couplings_embedding.astype(jnp.float32) + pair_update * keep[:, None, None] * keep[None, :, None]
    return (alignment_refreshed, couplings_refreshed.astype(jnp.bfloat16))
```

```python
import jax
import jax.numpy as jnp
import numpy as np
from jax import lax
from jax.experimental import pallas as pl
from jax.experimental.pallas import tpu as pltpu
from jax.sharding import PartitionSpec as P

F32 = jnp.float32
BF16 = jnp.bfloat16
HEADS = 8
HEAD = 32
SEQS = 4
ROWS = 192
QUADS = 48
COLS = 96
EMB = 256
PAIR = 128
PEERS_ROW = 8
PEERS_COL = 16
TOTAL = 1536
VMEM_LIMIT = 56 * 1024 * 1024


def mm(a, b):
    return jnp.dot(a, b, preferred_element_type=F32)


def mm_nt(a, b):
    return lax.dot_general(a, b, (((1,), (1,)), ((), ())), preferred_element_type=F32)


def mm_tn(a, b):
    return lax.dot_general(a, b, (((0,), (0,)), ((), ())), preferred_element_type=F32)


def normalised(x, gain):
    mean = jnp.mean(x, axis=-1, keepdims=True)
    d = x - mean
    var = jnp.mean(d * d, axis=-1, keepdims=True)
    return (d * lax.rsqrt(var + 1e-05) * gain).astype(BF16)


def slot_of(shape):
    return (lax.broadcasted_iota(jnp.int32, shape, len(shape) - 1) // HEAD) % 4


def params(**kw):
    return pltpu.CompilerParams(vmem_limit_bytes=VMEM_LIMIT, **kw)


def project_kernel(x_ref, g_ref, w_ref, e_ref, p_ref, qkv_ref, gate_ref):
    slot = slot_of((ROWS, 4 * 128))
    plain = [normalised(x_ref[s].astype(F32), g_ref[...]) for s in range(SEQS)]
    moved = [mm(p_ref[...], n).astype(BF16) for n in plain]
    for part in range(4):
        rows = moved if part in (0, 3) else plain
        for m in range(2):
            w = mm(w_ref[:, part * EMB + m * 128 : part * EMB + (m + 1) * 128], e_ref[...]).astype(BF16)
            acc = mm(rows[0], w)
            for s in range(1, SEQS):
                acc = jnp.where(slot == s, mm(rows[s], w), acc)
            for u in range(4):
                t = acc[:, u * 128 : (u + 1) * 128]
                h = 4 * m + u
                if part == 0:
                    qkv_ref[h, 0] = (t * HEAD ** (-0.5)).astype(BF16)
                elif part == 3:
                    gate_ref[h] = jax.nn.sigmoid(t)
                else:
                    qkv_ref[h, part] = t.astype(BF16)


def project(x, gain, w, expand, perm):
    return pl.pallas_call(
        project_kernel,
        out_shape=(
            jax.ShapeDtypeStruct((HEADS, 3, ROWS, 128), BF16),
            jax.ShapeDtypeStruct((HEADS, ROWS, 128), F32),
        ),
        compiler_params=params(),
        name="project",
    )(x, gain, w, expand, perm)


def bias_kernel(z_ref, g_ref, a_ref, o_ref):
    acc = jnp.zeros((128, 4 * COLS), F32)
    for k in range(8):
        n = normalised(z_ref[768 * k : 768 * (k + 1)].astype(F32), g_ref[...])
        both = jnp.concatenate([n[:384], n[384:]], axis=1)
        acc += mm_nt(a_ref[:, 256 * k : 256 * (k + 1)], both)
    o_ref[...] = acc.astype(BF16).reshape(HEADS, 16, 4 * COLS)


def pair_bias(z, gain, a):
    return pl.pallas_call(
        bias_kernel,
        out_shape=jax.ShapeDtypeStruct((HEADS, QUADS, 4 * COLS), BF16),
        grid=(3,),
        in_specs=[
            pl.BlockSpec((6144, PAIR), lambda t: (t, 0)),
            pl.BlockSpec((1, PAIR), lambda t: (0, 0)),
            pl.BlockSpec((128, 2048), lambda t: (0, 0)),
        ],
        out_specs=pl.BlockSpec((HEADS, 16, 4 * COLS), lambda t: (0, t, 0)),
        compiler_params=params(),
        name="pair_bias",
    )(z, gain, a)


def attend_kernel(qkv_ref, b_ref, m_ref, o_ref, k_ext, v_ext, bias):
    step = pl.program_id(0)
    block = 2 * ROWS

    @pl.when(step == 0)
    def _():
        slot = slot_of((ROWS, 128))
        eye = (
            lax.broadcasted_iota(jnp.int32, (8, 128), 0) == lax.broadcasted_iota(jnp.int32, (8, 128), 1)
        ).astype(BF16)
        absent = ((m_ref[...].astype(F32) - 1.0) * 1000000000.0).astype(BF16)
        k_ext[:, 128:] = mm_tn(absent, eye).astype(BF16)
        for r in range(PEERS_ROW):
            rows = slice(r * ROWS, (r + 1) * ROWS)
            k_ext[rows, :128] = qkv_ref[r, 1]
            v = qkv_ref[r, 2].astype(F32)
            for s in range(SEQS):
                v_ext[s, rows, :128] = jnp.where(slot == s, v, 0.0).astype(BF16)
                v_ext[s, rows, 128:] = jnp.where(slot == s, 1.0, 0.0).astype(BF16)

    for a in range(2):
        for quad in range(4):
            got = [b_ref[4 * quad + k, a].astype(F32) for k in range(4)]
            for u in range(4):
                line = jnp.concatenate([g[:, COLS * u : COLS * (u + 1)] for g in got], axis=1)
                bias[a * ROWS + u * QUADS : a * ROWS + (u + 1) * QUADS, 384 * quad : 384 * (quad + 1)] = line

    q = jnp.concatenate([qkv_ref[2 * step, 0], qkv_ref[2 * step + 1, 0]], axis=0).astype(F32)
    slot = slot_of((block, 128))
    lane = lax.broadcasted_iota(jnp.int32, (block, 128), 1)

    def one(s, total):
        lhs = jnp.concatenate(
            [jnp.where(slot == s, q, 0.0).astype(BF16), jnp.where(lane == s, 1.0, 0.0).astype(BF16)],
            axis=1,
        )
        scores = mm_nt(lhs, k_ext[...]) + bias[...]
        top = jnp.max(scores, axis=1, keepdims=True)
        e = jnp.exp(scores - top).astype(BF16)
        return total + mm(e, v_ext[s])

    total = lax.fori_loop(0, SEQS, one, jnp.zeros((block, 256), F32))
    o_ref[...] = (total[:, :128] / total[:, 128:]).astype(BF16).reshape(2, ROWS, 128)


def attend(qkv, bias, present):
    return pl.pallas_call(
        attend_kernel,
        out_shape=jax.ShapeDtypeStruct((PEERS_ROW, ROWS, 128), BF16),
        grid=(PEERS_ROW // 2,),
        in_specs=[
            pl.BlockSpec((PEERS_ROW, 3, ROWS, 128), lambda t: (0, 0, 0, 0)),
            pl.BlockSpec((PEERS_COL, 2, QUADS, 4 * COLS), lambda t: (0, t, 0, 0)),
            pl.BlockSpec((8, TOTAL), lambda t: (0, 0)),
        ],
        out_specs=pl.BlockSpec((2, ROWS, 128), lambda t: (t, 0, 0)),
        scratch_shapes=[
            pltpu.VMEM((TOTAL, 256), BF16),
            pltpu.VMEM((SEQS, TOTAL, 256), BF16),
            pltpu.VMEM((2 * ROWS, TOTAL), F32),
        ],
        compiler_params=params(),
        name="attend",
    )(qkv, bias, present)


def finish_kernel(
    att_ref, gate_ref, x_ref, wf_ref, pinv_ref, g_ref, wl_ref, wr_ref, ac_ref, ar_ref, new_ref, left_ref, right_ref
):
    gated = jnp.concatenate(
        [(gate_ref[h] * att_ref[h].astype(F32)).astype(BF16) for h in range(HEADS)], axis=1
    )
    gated = mm(pinv_ref[...], gated)
    w = jnp.concatenate([wf_ref[HEAD * (k // 4) : HEAD * (k // 4 + 1)] for k in range(4 * HEADS)], axis=0)
    slot = slot_of((ROWS, 4 * EMB))
    slot_one = slot_of((ROWS, 128))
    left = jnp.zeros((ROWS, 128), F32)
    for s in range(SEQS):
        inc = mm(jnp.where(slot == s, gated, 0.0).astype(BF16), w)
        new = (x_ref[s].astype(F32) + inc).astype(BF16)
        new_ref[s] = new
        n = normalised(new.astype(F32), g_ref[...])
        left = jnp.where(slot_one == s, mm(n, wl_ref[...]), left)
        right = mm_nt(wr_ref[...], n) * ar_ref[s : s + 1]
        right_ref[0, HEAD * s : HEAD * (s + 1)] = right[:, :COLS].astype(BF16)
        right_ref[1, HEAD * s : HEAD * (s + 1)] = right[:, COLS:].astype(BF16)
    left_ref[...] = (left * ac_ref[...]).astype(BF16)


def finish(*args):
    return pl.pallas_call(
        finish_kernel,
        out_shape=(
            jax.ShapeDtypeStruct((SEQS, ROWS, EMB), BF16),
            jax.ShapeDtypeStruct((ROWS, 128), BF16),
            jax.ShapeDtypeStruct((2, 128, COLS), BF16),
        ),
        compiler_params=params(),
        name="finish",
    )(*args)


STEP = 8


def outer_kernel(l_ref, r_ref, w_ref, off_ref, ki_ref, kj_ref, z_ref, o_ref, l_all, r_all, rhs_r, obf):
    step = pl.program_id(0)

    @pl.when(step == 0)
    def _():
        for c in range(PEERS_COL):
            l_all[ROWS * c : ROWS * (c + 1)] = l_ref[c].astype(F32)
            r_all[128 * c : 128 * (c + 1), :COLS] = r_ref[c].astype(F32)
        r_all[:, COLS:] = jnp.zeros((PEERS_COL * 128, 128 - COLS), F32)
        for q in range(8):
            lines = [
                r_all[pl.ds(HEAD * s + 4 * q + b, PEERS_COL, stride=128), :] for b in range(4) for s in range(SEQS)
            ]
            turned = jnp.transpose(jnp.concatenate(lines, axis=0))
            rhs_r[COLS * q : COLS * (q + 1)] = turned[:COLS].astype(BF16)

    slot = slot_of((PEERS_COL, 128))
    tiles = []
    for k in range(STEP):
        m = l_all[pl.ds(step * STEP + k, PEERS_COL, stride=ROWS), :]
        rolled = [m] + [pltpu.roll(m, HEAD * d, 1) for d in range(1, 4)]
        tiles.append(
            jnp.concatenate(
                [
                    jnp.where(slot == b, rolled[(b - s) % 4], 0.0).astype(BF16)
                    for b in range(4)
                    for s in range(SEQS)
                ],
                axis=0,
            )
        )
    for k in range(0, STEP, 2):
        outer = mm(rhs_r[...], jnp.concatenate(tiles[k : k + 2], axis=1)).astype(BF16)
        for e in range(2):
            for q in range(8):
                obf[COLS * (k + e) : COLS * (k + e + 1), 128 * q : 128 * (q + 1)] = outer[
                    COLS * q : COLS * (q + 1), 128 * e : 128 * (e + 1)
                ]
    update = mm(obf[...], w_ref[...]) + off_ref[...]
    for k in range(STEP):
        keep = kj_ref[...] * ki_ref[step * STEP + k]
        o_ref[k] = (z_ref[k].astype(F32) + update[COLS * k : COLS * (k + 1)] * keep).astype(BF16)


def outer_update(left, right, w, offset, keep_i, keep_j, z):
    return pl.pallas_call(
        outer_kernel,
        out_shape=jax.ShapeDtypeStruct((ROWS, COLS, PAIR), BF16),
        grid=(ROWS // STEP,),
        in_specs=[
            pl.BlockSpec((PEERS_COL, ROWS, 128), lambda t: (0, 0, 0)),
            pl.BlockSpec((PEERS_COL, 128, COLS), lambda t: (0, 0, 0)),
            pl.BlockSpec((1024, PAIR), lambda t: (0, 0)),
            pl.BlockSpec((1, PAIR), lambda t: (0, 0)),
            pl.BlockSpec(memory_space=pltpu.SMEM),
            pl.BlockSpec((COLS, PAIR), lambda t: (0, 0)),
            pl.BlockSpec((STEP, COLS, PAIR), lambda t: (t, 0, 0)),
        ],
        out_specs=pl.BlockSpec((STEP, COLS, PAIR), lambda t: (t, 0, 0)),
        scratch_shapes=[
            pltpu.VMEM((PEERS_COL * ROWS, 128), F32),
            pltpu.VMEM((PEERS_COL * 128, 128), F32),
            pltpu.VMEM((8 * COLS, 256), BF16),
            pltpu.VMEM((STEP * COLS, 1024), BF16),
        ],
        compiler_params=params(),
        name="outer_update",
    )(left, right, w, offset, keep_i, keep_j, z)


def tables():
    expand = np.zeros((128, 4, 4, HEAD), np.float32)
    for u in range(4):
        for d in range(HEAD):
            expand[u * HEAD + d, u, :, d] = 1
    perm = np.zeros((ROWS, ROWS), np.float32)
    for i in range(ROWS):
        perm[(i % 4) * QUADS + i // 4, i] = 1
    return expand.reshape(128, 512), perm


def on_device(
    alignment_embedding,
    couplings_embedding,
    alignment_availability,
    amino_availability,
    alignment_scaling_vector,
    attention_joint_matrix,
    attention_final_matrix,
    coupling_scaling_vector,
    coupling_logit_matrix,
    tensor_scaling_vector,
    first_factor_matrix,
    second_factor_matrix,
    tensor_projection_matrix,
    tensor_offset_vector,
):
    expand, perm = tables()
    qkv, gate = project(
        alignment_embedding,
        alignment_scaling_vector[None],
        attention_joint_matrix,
        jnp.asarray(expand, BF16),
        jnp.asarray(perm, BF16),
    )
    qkv = lax.all_to_all(qkv, "row", 0, 0, tiled=True)
    spread = (
        jnp.eye(16, dtype=BF16)[None, :, :, None] * coupling_logit_matrix.T[:, None, None, :]
    ).reshape(HEADS * 16, 16 * PAIR)
    bias = pair_bias(
        couplings_embedding.reshape(ROWS * COLS, PAIR), coupling_scaling_vector[None], spread
    )
    bias = lax.all_to_all(bias, "row", 0, 0, tiled=True)
    bias = lax.all_gather(bias, "col", axis=0)
    present = jnp.pad(alignment_availability.astype(BF16), ((0, 4), (0, 0)))
    present_all = lax.all_gather(present, "row", axis=1, tiled=True)
    attended = attend(qkv, bias, present_all)
    attended = lax.all_to_all(attended, "row", 0, 0, tiled=True)
    present = alignment_availability.astype(F32)
    alignment_refreshed, left, right = finish(
        attended,
        gate,
        alignment_embedding,
        attention_final_matrix,
        jnp.asarray(perm.T, BF16),
        tensor_scaling_vector[None],
        jnp.tile(first_factor_matrix, (1, 4)),
        second_factor_matrix.T,
        jnp.repeat(present.T, HEAD, axis=1),
        present,
    )
    left = lax.all_gather(left, "col", axis=0)
    right = lax.all_gather(right, "row", axis=0, tiled=True)
    right = lax.all_to_all(right, "col", 0, 0, tiled=True)
    keep = amino_availability.astype(F32)
    keep_i = lax.dynamic_slice_in_dim(keep, lax.axis_index("row") * ROWS, ROWS)
    keep_j = lax.dynamic_slice_in_dim(keep, lax.axis_index("col") * COLS, COLS)
    projection = (tensor_projection_matrix.astype(F32) / 64).astype(BF16)
    projection = projection.reshape(HEAD, 8, 4, PAIR).transpose(1, 2, 0, 3).reshape(1024, PAIR)
    couplings_refreshed = outer_update(
        left,
        right,
        projection,
        tensor_offset_vector[None],
        keep_i,
        jnp.broadcast_to(keep_j[:, None], (COLS, PAIR)),
        couplings_embedding,
    )
    return alignment_refreshed, couplings_refreshed


def solution(mesh):
    placed = (P("col", "row", None), P("row", "col", None), P("col", "row")) + (P(),) * 11
    return jax.shard_map(
        on_device,
        mesh=mesh,
        in_specs=placed,
        out_specs=(P("col", "row", None), P("row", "col", None)),
        check_vma=False,
    )
```

```python
import jax
import jax.numpy as jnp
import numpy as np
from jax import lax
from jax.experimental import pallas as pl
from jax.experimental.pallas import tpu as pltpu
from jax.sharding import Mesh, PartitionSpec as P

F32 = jnp.float32
BF16 = jnp.bfloat16
HEADS = 8
HEAD = 32
SEQS = 4
ROWS = 192
HALF = 96
QUADS = 24
COLS = 96
EMB = 256
PAIR = 128
PEERS_COL = 16
TOTAL = 1536
CHUNK = 4
Q_ROWS, K_ROWS, V_ROWS, M_ROWS = 0, 192, 384, 576
SENT_ROWS = 592
LOG2E = 1.4426950408889634
ROW = ("x", "zl")
COL = ("y", "zh", "core")
VMEM_LIMIT = 56 * 1024 * 1024


def mm(a, b):
    return jnp.dot(a, b, preferred_element_type=F32)


def mm_nt(a, b):
    return lax.dot_general(a, b, (((1,), (1,)), ((), ())), preferred_element_type=F32)


def normalised(x, gain):
    mean = jnp.mean(x, axis=-1, keepdims=True)
    d = x - mean
    var = jnp.mean(d * d, axis=-1, keepdims=True)
    return (d * lax.rsqrt(var + 1e-05) * gain).astype(BF16)


def slot_of(shape):
    return (lax.broadcasted_iota(jnp.int32, shape, len(shape) - 1) // HEAD) % 4


def params():
    return pltpu.CompilerParams(vmem_limit_bytes=VMEM_LIMIT)


def vmem():
    return pl.BlockSpec(memory_space=pltpu.VMEM)


def smem():
    return pl.BlockSpec(memory_space=pltpu.SMEM)


def project_kernel(x_ref, g_ref, w_ref, e_ref, p_ref, m_ref, qkv_ref, gate_ref):
    slot = slot_of((ROWS, 4 * 128))
    plain = [normalised(x_ref[s].astype(F32), g_ref[...]) for s in range(SEQS)]
    moved = [mm(p_ref[...], n).astype(BF16) for n in plain]
    for part in range(4):
        rows = moved if part in (0, 3) else plain
        for m in range(2):
            w = mm(w_ref[:, part * EMB + m * 128 : part * EMB + (m + 1) * 128], e_ref[...]).astype(BF16)
            acc = mm(rows[0], w)
            for s in range(1, SEQS):
                acc = jnp.where(slot == s, mm(rows[s], w), acc)
            for u in range(4):
                t = acc[:, u * 128 : (u + 1) * 128]
                h = 4 * m + u
                if part == 0:
                    qkv_ref[h, Q_ROWS:K_ROWS] = (t * HEAD ** (-0.5)).astype(BF16)
                elif part == 1:
                    qkv_ref[h, K_ROWS:V_ROWS] = t.astype(BF16)
                elif part == 2:
                    qkv_ref[h, V_ROWS:M_ROWS] = t.astype(BF16)
                else:
                    gate_ref[h] = jax.nn.sigmoid(t)
    for h in range(HEADS):
        qkv_ref[h, M_ROWS:] = m_ref[...]


def project(x, gain, w, expand, perm, present):
    return pl.pallas_call(
        project_kernel,
        out_shape=(
            jax.ShapeDtypeStruct((HEADS, SENT_ROWS, 128), BF16),
            jax.ShapeDtypeStruct((HEADS, ROWS, 128), F32),
        ),
        compiler_params=params(),
        name="project",
    )(x, gain, w, expand, perm, present)


def bias_kernel(z_ref, g_ref, a_ref, o_ref):
    acc = jnp.zeros((128, 4 * COLS), F32)
    for k in range(8):
        n = normalised(z_ref[768 * k : 768 * (k + 1)].astype(F32), g_ref[...])
        both = jnp.concatenate([n[:384], n[384:]], axis=1)
        acc += mm_nt(a_ref[:, 256 * k : 256 * (k + 1)], both)
    o_ref[...] = acc.astype(BF16).reshape(HEADS, 16, 4 * COLS)


def pair_bias(z, gain, a):
    return pl.pallas_call(
        bias_kernel,
        out_shape=jax.ShapeDtypeStruct((HEADS, 2 * QUADS, 4 * COLS), BF16),
        grid=(3,),
        in_specs=[
            pl.BlockSpec((6144, PAIR), lambda t: (t, 0)),
            pl.BlockSpec((1, PAIR), lambda t: (0, 0)),
            pl.BlockSpec((128, 2048), lambda t: (0, 0)),
        ],
        out_specs=pl.BlockSpec((HEADS, 16, 4 * COLS), lambda t: (0, t, 0)),
        compiler_params=params(),
        name="pair_bias",
    )(z, gain, a)


OFFSETS = (0, 3, 1, 2)


def prepare_kernel(at_ref, own_ref, par_ref, k_ref, v_ref, q_ref):
    y = at_ref[0]
    core = at_ref[1]
    for side, ref in enumerate((own_ref, par_ref)):
        for d in range(4):
            first = 2 * lax.rem(y + OFFSETS[d], 4)
            span = slice(384 * d, 384 * (d + 1))
            keys = jnp.concatenate([ref[first + e, K_ROWS:V_ROWS] for e in range(2)], axis=0)
            k_ref[side, :128, span] = jnp.transpose(keys.astype(F32)).astype(BF16)
            for e in range(2):
                v_ref[side, 384 * d + ROWS * e : 384 * d + ROWS * (e + 1), :128] = ref[first + e, V_ROWS:M_ROWS]
            masks = [ref[first + e, M_ROWS:].astype(F32) for e in range(2)]
            line = jnp.concatenate([masks[0][:8], masks[0][8:, :64], masks[1][:8], masks[1][8:, :64]], axis=1)
            absent = (line - 1.0) * 1000000000.0
            k_ref[side, 128:, span] = jnp.concatenate([absent, jnp.zeros((120, 384), F32)], axis=0).astype(BF16)
        v_ref[side, :, 128:] = jnp.ones((TOTAL, 128), BF16)
        for r in range(8):
            q_ref[side, r] = ref[r, pl.ds(pl.multiple_of(core * HALF, HALF), HALF)]


def prepare(at, own, par):
    return pl.pallas_call(
        prepare_kernel,
        out_shape=(
            jax.ShapeDtypeStruct((2, EMB, TOTAL), BF16),
            jax.ShapeDtypeStruct((2, TOTAL, EMB), BF16),
            jax.ShapeDtypeStruct((2, 8, HALF, 128), BF16),
        ),
        in_specs=[smem(), vmem(), vmem()],
        out_specs=(vmem(), vmem(), vmem()),
        compiler_params=params(),
        name="prepare",
    )(at, own, par)


def attend_kernel(at_ref, k_ref, v_ref, q_ref, b0, bp, bm, f1, f2, o_ref, bias, even, odd):
    core = at_ref[1]
    count = CHUNK * HALF
    for d, ref in enumerate((b0, bp, bm, (f1, f2))):
        for r in range(CHUNK):
            got = ref[r] if d < 3 else ref[r // 2][r % 2]
            got = [got[k].astype(F32) * LOG2E for k in range(4)]
            for u in range(4):
                line = jnp.concatenate([g[:, COLS * u : COLS * (u + 1)] for g in got], axis=1)
                top = r * HALF + u * QUADS
                bias[top : top + QUADS, 384 * d : 384 * (d + 1)] = line
    slot = slot_of((count, 128))
    wide = slot_of((count, 256))
    lane = lax.broadcasted_iota(jnp.int32, (count, 128), 1)

    def scores(out, side, s):
        q = jnp.concatenate([q_ref[side, r] for r in range(CHUNK)], axis=0).astype(F32)
        lhs = jnp.concatenate(
            [jnp.where(slot == s, q, 0.0).astype(BF16), jnp.where(lane == s, 1.0, 0.0).astype(BF16)], axis=1
        )
        top = None
        for t in range(6):
            span = slice(256 * t, 256 * (t + 1))
            c = mm(lhs, k_ref[side, :, span]) * LOG2E + bias[:, span]
            out[:, span] = c
            both = jnp.maximum(c[:, :128], c[:, 128:])
            top = both if top is None else jnp.maximum(top, both)
        return jnp.max(top, axis=1, keepdims=True)

    def values(buf, top, side):
        acc = None
        for t in range(6):
            span = slice(256 * t, 256 * (t + 1))
            e = jnp.exp2(buf[:, span] - top).astype(BF16)
            p = mm(e, v_ref[side, span])
            acc = p if acc is None else acc + p
        return acc

    for side in range(2):
        top = scores(even, side, 0)
        total = jnp.zeros((count, 256), F32)
        for s in range(SEQS):
            now, later = (even, odd) if s % 2 == 0 else (odd, even)
            if s < SEQS - 1:
                following = scores(later, side, s + 1)
            total = jnp.where(wide == s, values(now, top, side), total)
            if s < SEQS - 1:
                top = following
        out = (total[:, :128] / total[:, 128:]).astype(BF16)
        quad = core if side == 0 else 1 - core
        for r in range(CHUNK):
            o_ref[r, quad] = out[HALF * r : HALF * (r + 1)]


def attend(at, k, v, q, pieces, chunk):
    return pl.pallas_call(
        attend_kernel,
        out_shape=jax.ShapeDtypeStruct((CHUNK, 2, HALF, 128), BF16),
        grid=(1,),
        in_specs=[
            smem(),
            pl.BlockSpec((2, EMB, TOTAL), lambda t: (0, 0, 0)),
            pl.BlockSpec((2, TOTAL, EMB), lambda t: (0, 0, 0)),
            pl.BlockSpec((2, CHUNK, HALF, 128), lambda t: (0, chunk, 0, 0)),
        ]
        + [vmem()] * 5,
        out_specs=pl.BlockSpec((CHUNK, 2, HALF, 128), lambda t: (0, 0, 0, 0)),
        scratch_shapes=[pltpu.VMEM((CHUNK * HALF, TOTAL), F32) for _ in range(3)],
        compiler_params=params(),
        name=f"attend_{chunk}",
    )(at, k, v, q, *pieces)


def finish_kernel(
    att_ref, gate_ref, x_ref, wf_ref, pinv_ref, g_ref, wl_ref, wr_ref, ac_ref, ar_ref, new_ref, left_ref, right_ref
):
    gated = jnp.concatenate(
        [(gate_ref[h] * att_ref[h].astype(F32)).astype(BF16) for h in range(HEADS)], axis=1
    )
    gated = mm(pinv_ref[...], gated)
    w = jnp.concatenate([wf_ref[HEAD * (k // 4) : HEAD * (k // 4 + 1)] for k in range(4 * HEADS)], axis=0)
    slot = slot_of((ROWS, 4 * EMB))
    slot_one = slot_of((ROWS, 128))
    left = jnp.zeros((ROWS, 128), F32)
    for s in range(SEQS):
        inc = mm(jnp.where(slot == s, gated, 0.0).astype(BF16), w)
        new = (x_ref[s].astype(F32) + inc).astype(BF16)
        new_ref[s] = new
        n = normalised(new.astype(F32), g_ref[...])
        left = jnp.where(slot_one == s, mm(n, wl_ref[...]), left)
        right = mm_nt(wr_ref[...], n) * ar_ref[s : s + 1]
        rows = slice(HEAD * s, HEAD * (s + 1))
        right_ref[0, rows] = right[:, :128].astype(BF16)
        right_ref[1, rows] = jnp.concatenate([right[:, COLS:], right[:, :32]], axis=1).astype(BF16)
    left_ref[...] = (left * ac_ref[...]).astype(BF16)


def finish(*args):
    return pl.pallas_call(
        finish_kernel,
        out_shape=(
            jax.ShapeDtypeStruct((SEQS, ROWS, EMB), BF16),
            jax.ShapeDtypeStruct((ROWS, 128), BF16),
            jax.ShapeDtypeStruct((2, 128, 128), BF16),
        ),
        compiler_params=params(),
        name="finish",
    )(*args)


STEP = 48


def outer_kernel(at_ref, lo_ref, lp_ref, r_ref, w_ref, off_ref, ki_ref, kj_ref, z_ref, o_ref, l_all, r_all, lhs, rhs, obf):
    step = pl.program_id(0)

    @pl.when(step == 0)
    def _():
        core = at_ref[1]
        for p in range(PEERS_COL // 2):
            for side, ref in enumerate((lo_ref, lp_ref)):
                c = 2 * p + (core if side == 0 else 1 - core)
                l_all[pl.ds(pl.multiple_of(c * ROWS, ROWS), ROWS)] = ref[p].astype(F32)
        for c in range(PEERS_COL):
            r_all[128 * c : 128 * (c + 1)] = r_ref[c].astype(F32)
        for q in range(8):
            lines = [
                r_all[pl.ds(HEAD * s + 4 * q + b, PEERS_COL, stride=128), :] for b in range(4) for s in range(SEQS)
            ]
            turned = jnp.transpose(jnp.concatenate(lines, axis=0))
            lhs[COLS * q : COLS * (q + 1)] = turned[:COLS].astype(BF16)

    slot = slot_of((PEERS_COL, 128))
    for k in range(STEP):
        m = l_all[pl.ds(step * STEP + k, PEERS_COL, stride=ROWS), :]
        rolled = [m] + [pltpu.roll(m, HEAD * d, 1) for d in range(1, 4)]
        for b in range(4):
            for s in range(SEQS):
                at = 64 * b + 16 * s
                rhs[at : at + 16, 128 * k : 128 * (k + 1)] = jnp.where(slot == b, rolled[(b - s) % 4], 0.0).astype(BF16)
    for k in range(0, STEP, 2):
        outer = mm(lhs[...], rhs[:, 128 * k : 128 * (k + 2)]).astype(BF16)
        for e in range(2):
            for q in range(8):
                obf[COLS * (k + e) : COLS * (k + e + 1), 128 * q : 128 * (q + 1)] = outer[
                    COLS * q : COLS * (q + 1), 128 * e : 128 * (e + 1)
                ]
    update = mm(obf[...], w_ref[...]) + off_ref[...]
    for k in range(STEP):
        keep = kj_ref[...] * ki_ref[step * STEP + k]
        o_ref[k] = (z_ref[k].astype(F32) + update[COLS * k : COLS * (k + 1)] * keep).astype(BF16)


def outer_update(at, left_own, left_par, right, w, offset, keep_i, keep_j, z):
    return pl.pallas_call(
        outer_kernel,
        out_shape=jax.ShapeDtypeStruct((ROWS, COLS, PAIR), BF16),
        grid=(ROWS // STEP,),
        in_specs=[
            smem(),
            pl.BlockSpec((PEERS_COL // 2, ROWS, 128), lambda t: (0, 0, 0)),
            pl.BlockSpec((PEERS_COL // 2, ROWS, 128), lambda t: (0, 0, 0)),
            pl.BlockSpec((PEERS_COL, 128, 128), lambda t: (0, 0, 0)),
            pl.BlockSpec((1024, PAIR), lambda t: (0, 0)),
            pl.BlockSpec((1, PAIR), lambda t: (0, 0)),
            smem(),
            pl.BlockSpec((COLS, PAIR), lambda t: (0, 0)),
            pl.BlockSpec((STEP, COLS, PAIR), lambda t: (t, 0, 0)),
        ],
        out_specs=pl.BlockSpec((STEP, COLS, PAIR), lambda t: (t, 0, 0)),
        scratch_shapes=[
            pltpu.VMEM((PEERS_COL * ROWS, 128), F32),
            pltpu.VMEM((PEERS_COL * 128, 128), F32),
            pltpu.VMEM((8 * COLS, 256), BF16),
            pltpu.VMEM((256, 128 * STEP), BF16),
            pltpu.VMEM((STEP * COLS, 1024), BF16),
        ],
        compiler_params=params(),
        name="outer_update",
    )(at, left_own, left_par, right, w, offset, keep_i, keep_j, z)


def tables():
    expand = np.zeros((128, 4, 4, HEAD), np.float32)
    for u in range(4):
        for d in range(HEAD):
            expand[u * HEAD + d, u, :, d] = 1
    perm = np.zeros((ROWS, ROWS), np.float32)
    for i in range(ROWS):
        half, rest = divmod(i, HALF)
        perm[half * HALF + (rest % 4) * QUADS + rest // 4, i] = 1
    return expand.reshape(128, 512), perm


def swap_cores(x):
    return lax.ppermute(x, "core", [(0, 1), (1, 0)])


def along_y(x, d):
    return lax.ppermute(x, "y", [(a, (a + d) % 4) for a in range(4)])


def to_all(x, axes, n):
    return lax.all_to_all(jnp.broadcast_to(x[None], (n,) + x.shape), axes, 0, 0, tiled=True)


def turn_grid(x):
    def index(a, b, c, d):
        return ((a * 2 + b) * 4 + c) * 2 + d

    moves = [
        (index(a, b, c, d), index(c, d, a, b)) for a in range(4) for b in range(2) for c in range(4) for d in range(2)
    ]
    return lax.ppermute(x, ("x", "zl", "y", "zh"), moves)


def ring_pieces(block):
    up, down = along_y(block, 1), along_y(block, 3)
    return block, up, down, along_y(up[: CHUNK // 2], 1), along_y(down[CHUNK // 2 :], 3)


def on_device(
    alignment_embedding,
    couplings_embedding,
    alignment_availability,
    amino_availability,
    alignment_scaling_vector,
    attention_joint_matrix,
    attention_final_matrix,
    coupling_scaling_vector,
    coupling_logit_matrix,
    tensor_scaling_vector,
    first_factor_matrix,
    second_factor_matrix,
    tensor_projection_matrix,
    tensor_offset_vector,
):
    core = lax.axis_index("core")
    at = jnp.stack([lax.axis_index("y"), core]).astype(jnp.int32)
    expand, perm = tables()

    spread = (
        jnp.eye(16, dtype=BF16)[None, :, :, None] * coupling_logit_matrix.T[:, None, None, :]
    ).reshape(HEADS * 16, 16 * PAIR)
    bias = pair_bias(
        couplings_embedding.reshape(ROWS * COLS, PAIR), coupling_scaling_vector[None], spread
    ).reshape(HEADS, 1, 2, QUADS, 4 * COLS)
    bias = jnp.broadcast_to(bias, (HEADS, 2, 2, QUADS, 4 * COLS)).reshape(4 * HEADS, QUADS, 4 * COLS)
    bias = lax.all_to_all(bias, ROW + ("zh", "core"), 0, 0, tiled=True).reshape(8, 4, QUADS, 4 * COLS)

    present = alignment_availability.astype(BF16)
    sent_mask = jnp.pad(
        jnp.stack([present[:, :128], jnp.pad(present[:, 128:], ((0, 0), (0, 64)))]), ((0, 0), (0, 4), (0, 0))
    ).reshape(16, 128)
    own, gate = project(
        alignment_embedding,
        alignment_scaling_vector[None],
        attention_joint_matrix,
        jnp.asarray(expand, BF16),
        jnp.asarray(perm, BF16),
        sent_mask,
    )
    own = lax.all_to_all(own, ROW, 0, 0, tiled=True)
    k, v, q = prepare(at, own, swap_cores(own))

    attended = jnp.concatenate(
        [attend(at, k, v, q, ring_pieces(bias[CHUNK * c : CHUNK * (c + 1)]), c) for c in range(2)], axis=0
    ).reshape(16, HALF, 128)
    attended = lax.all_to_all(attended, ROW + ("core",), 0, 0, tiled=True).reshape(HEADS, ROWS, 128)

    present = alignment_availability.astype(F32)
    alignment_refreshed, left, right = finish(
        attended,
        gate,
        alignment_embedding,
        attention_final_matrix,
        jnp.asarray(perm.T, BF16),
        tensor_scaling_vector[None],
        jnp.tile(first_factor_matrix, (1, 4)),
        second_factor_matrix.T,
        jnp.repeat(present.T, HEAD, axis=1),
        present,
    )
    mine = lax.dynamic_index_in_dim(right, core, 0, False)
    theirs = swap_cores(lax.dynamic_index_in_dim(right, 1 - core, 0, False))
    right = jnp.where(core == 0, jnp.stack([mine, theirs]), jnp.stack([theirs, mine]))
    right = to_all(turn_grid(right), ROW, 8).reshape(PEERS_COL, 128, 128)
    left = to_all(left, ("y", "zh"), 8)

    keep = amino_availability.astype(F32)
    keep_i = lax.dynamic_slice_in_dim(keep, lax.axis_index(ROW) * ROWS, ROWS)
    keep_j = lax.dynamic_slice_in_dim(keep, lax.axis_index(COL) * COLS, COLS)
    projection = (tensor_projection_matrix.astype(F32) / 64).astype(BF16)
    projection = projection.reshape(HEAD, 8, 4, PAIR).transpose(1, 2, 0, 3).reshape(1024, PAIR)
    couplings_refreshed = outer_update(
        at,
        left,
        swap_cores(left),
        right,
        projection,
        tensor_offset_vector[None],
        keep_i,
        jnp.broadcast_to(keep_j[:, None], (COLS, PAIR)),
        couplings_embedding,
    )
    return alignment_refreshed, couplings_refreshed


def solution(mesh):
    mesh = Mesh(mesh.devices.reshape(4, 2, 4, 2, 2), ROW + COL)
    placed = (P(COL, ROW, None), P(ROW, COL, None), P(COL, ROW)) + (P(),) * 11
    return jax.shard_map(
        on_device,
        mesh=mesh,
        in_specs=placed,
        out_specs=(P(COL, ROW, None), P(ROW, COL, None)),
        check_vma=False,
    )
```

```python
import jax
import jax.numpy as jnp
import numpy as np
from jax import lax
from jax.experimental import pallas as pl
from jax.experimental.pallas import tpu as pltpu
from jax.sharding import Mesh, PartitionSpec as P

F32 = jnp.float32
BF16 = jnp.bfloat16
HEADS = 8
HEAD = 32
SEQS = 4
ROWS = 192
HALF = 96
QUADS = 24
COLS = 96
EMB = 256
PAIR = 128
PEERS_COL = 16
TOTAL = 1536
CHUNK = 4
Q_ROWS, K_ROWS, V_ROWS, M_ROWS = 0, 192, 384, 576
SENT_ROWS = 592
LOG2E = 1.4426950408889634
ROW = ("x", "zl")
COL = ("y", "zh", "core")
VMEM_LIMIT = 56 * 1024 * 1024


def mm(a, b):
    return jnp.dot(a, b, preferred_element_type=F32)


def mm_nt(a, b):
    return lax.dot_general(a, b, (((1,), (1,)), ((), ())), preferred_element_type=F32)


def normalised(x, gain):
    mean = jnp.mean(x, axis=-1, keepdims=True)
    d = x - mean
    var = jnp.mean(d * d, axis=-1, keepdims=True)
    return (d * lax.rsqrt(var + 1e-05) * gain).astype(BF16)


def slot_of(shape):
    return (lax.broadcasted_iota(jnp.int32, shape, len(shape) - 1) // HEAD) % 4


def params():
    return pltpu.CompilerParams(vmem_limit_bytes=VMEM_LIMIT)


def vmem():
    return pl.BlockSpec(memory_space=pltpu.VMEM)


def smem():
    return pl.BlockSpec(memory_space=pltpu.SMEM)


def project_kernel(x_ref, g_ref, w_ref, e_ref, p_ref, m_ref, qkv_ref, gate_ref):
    slot = slot_of((ROWS, 4 * 128))
    plain = [normalised(x_ref[s].astype(F32), g_ref[...]) for s in range(SEQS)]
    moved = [mm(p_ref[...], n).astype(BF16) for n in plain]
    for part in range(4):
        rows = moved if part in (0, 3) else plain
        for m in range(2):
            w = mm(w_ref[:, part * EMB + m * 128 : part * EMB + (m + 1) * 128], e_ref[...]).astype(BF16)
            acc = mm(rows[0], w)
            for s in range(1, SEQS):
                acc = jnp.where(slot == s, mm(rows[s], w), acc)
            for u in range(4):
                t = acc[:, u * 128 : (u + 1) * 128]
                h = 4 * m + u
                if part == 0:
                    qkv_ref[h, Q_ROWS:K_ROWS] = (t * HEAD ** (-0.5)).astype(BF16)
                elif part == 1:
                    qkv_ref[h, K_ROWS:V_ROWS] = t.astype(BF16)
                elif part == 2:
                    qkv_ref[h, V_ROWS:M_ROWS] = t.astype(BF16)
                else:
                    gate_ref[h] = jax.nn.sigmoid(t)
    for h in range(HEADS):
        qkv_ref[h, M_ROWS:] = m_ref[...]


def project(x, gain, w, expand, perm, present):
    return pl.pallas_call(
        project_kernel,
        out_shape=(
            jax.ShapeDtypeStruct((HEADS, SENT_ROWS, 128), BF16),
            jax.ShapeDtypeStruct((HEADS, ROWS, 128), F32),
        ),
        compiler_params=params(),
        name="project",
    )(x, gain, w, expand, perm, present)


def bias_kernel(z_ref, g_ref, w_ref, o_ref):
    acc = jnp.zeros((128, 4 * COLS), F32)
    group = lax.broadcasted_iota(jnp.int32, (128, PAIR), 0) % 16
    w = w_ref[...].astype(F32)
    for k in range(8):
        n = normalised(z_ref[768 * k : 768 * (k + 1)].astype(F32), g_ref[...])
        both = jnp.concatenate([n[:384], n[384:]], axis=1)
        spread = [jnp.where(group == 2 * k + e, w, 0.0).astype(BF16) for e in range(2)]
        acc += mm_nt(jnp.concatenate(spread, axis=1), both)
    out = acc.astype(BF16).reshape(HEADS, 16, 4 * COLS)
    for copy in range(2):
        o_ref[:, copy] = out


def pair_bias(z, gain, w):
    return pl.pallas_call(
        bias_kernel,
        out_shape=jax.ShapeDtypeStruct((HEADS, 2, 2 * QUADS, 4 * COLS), BF16),
        grid=(3,),
        in_specs=[
            pl.BlockSpec((6144, PAIR), lambda t: (t, 0)),
            pl.BlockSpec((1, PAIR), lambda t: (0, 0)),
            pl.BlockSpec((128, PAIR), lambda t: (0, 0)),
        ],
        out_specs=pl.BlockSpec((HEADS, 2, 16, 4 * COLS), lambda t: (0, 0, t, 0)),
        compiler_params=params(),
        name="pair_bias",
    )(z, gain, w)


OFFSETS = (0, 3, 1, 2)


def prepare_kernel(at_ref, own_ref, par_ref, k_ref, v_ref, q_ref):
    y = at_ref[0]
    core = at_ref[1]
    for side, ref in enumerate((own_ref, par_ref)):
        for d in range(4):
            first = 2 * lax.rem(y + OFFSETS[d], 4)
            span = slice(384 * d, 384 * (d + 1))
            keys = jnp.concatenate([ref[first + e, K_ROWS:V_ROWS] for e in range(2)], axis=0)
            k_ref[side, :128, span] = jnp.transpose(keys.astype(F32)).astype(BF16)
            for e in range(2):
                v_ref[side, 384 * d + ROWS * e : 384 * d + ROWS * (e + 1), :128] = ref[first + e, V_ROWS:M_ROWS]
            masks = [ref[first + e, M_ROWS:].astype(F32) for e in range(2)]
            line = jnp.concatenate([masks[0][:8], masks[0][8:, :64], masks[1][:8], masks[1][8:, :64]], axis=1)
            absent = (line - 1.0) * 1000000000.0
            k_ref[side, 128:, span] = jnp.concatenate([absent, jnp.zeros((120, 384), F32)], axis=0).astype(BF16)
        v_ref[side, :, 128:] = jnp.ones((TOTAL, 128), BF16)
        for r in range(8):
            q_ref[side, r] = ref[r, pl.ds(pl.multiple_of(core * HALF, HALF), HALF)]


def prepare(at, own, par):
    return pl.pallas_call(
        prepare_kernel,
        out_shape=(
            jax.ShapeDtypeStruct((2, EMB, TOTAL), BF16),
            jax.ShapeDtypeStruct((2, TOTAL, EMB), BF16),
            jax.ShapeDtypeStruct((2, 8, HALF, 128), BF16),
        ),
        in_specs=[smem(), vmem(), vmem()],
        out_specs=(vmem(), vmem(), vmem()),
        compiler_params=params(),
        name="prepare",
    )(at, own, par)


def attend_kernel(at_ref, k_ref, v_ref, q_ref, b0, bp, bm, f1, f2, o_ref, bias, even, odd):
    core = at_ref[1]
    count = CHUNK * HALF
    for d, refs in enumerate(((b0,), (bp,), (bm,), (f1, f2))):
        for r in range(CHUNK):
            got = [ref[r, k].astype(F32) * LOG2E for ref in refs for k in range(4 // len(refs))]
            for u in range(4):
                line = jnp.concatenate([g[:, COLS * u : COLS * (u + 1)] for g in got], axis=1)
                top = r * HALF + u * QUADS
                bias[top : top + QUADS, 384 * d : 384 * (d + 1)] = line
    slot = slot_of((count, 128))
    wide = slot_of((count, 256))
    lane = lax.broadcasted_iota(jnp.int32, (count, 128), 1)

    def scores(out, side, s):
        q = jnp.concatenate([q_ref[side, r] for r in range(CHUNK)], axis=0).astype(F32)
        lhs = jnp.concatenate(
            [jnp.where(slot == s, q, 0.0).astype(BF16), jnp.where(lane == s, 1.0, 0.0).astype(BF16)], axis=1
        )
        top = None
        for t in range(6):
            span = slice(256 * t, 256 * (t + 1))
            c = mm(lhs, k_ref[side, :, span]) * LOG2E + bias[:, span]
            out[:, span] = c
            both = jnp.maximum(c[:, :128], c[:, 128:])
            top = both if top is None else jnp.maximum(top, both)
        return jnp.max(top, axis=1, keepdims=True)

    def values(buf, top, side):
        acc = None
        for t in range(6):
            span = slice(256 * t, 256 * (t + 1))
            e = jnp.exp2(buf[:, span] - top).astype(BF16)
            p = mm(e, v_ref[side, span])
            acc = p if acc is None else acc + p
        return acc

    top = scores(even, 0, 0)
    for n in range(2 * SEQS):
        side, s = divmod(n, SEQS)
        now, later = (even, odd) if n % 2 == 0 else (odd, even)
        if n < 2 * SEQS - 1:
            following = scores(later, *divmod(n + 1, SEQS))
        got = values(now, top, side)
        total = got if s == 0 else jnp.where(wide == s, got, total)
        if n < 2 * SEQS - 1:
            top = following
        if s == SEQS - 1:
            out = (total[:, :128] / total[:, 128:]).astype(BF16)
            quad = core if side == 0 else 1 - core
            for r in range(CHUNK):
                o_ref[r, quad] = out[HALF * r : HALF * (r + 1)]


def attend(at, k, v, q, pieces):
    def piece(parts):
        return pl.BlockSpec((CHUNK, parts, QUADS, 4 * COLS), lambda t: (t, 0, 0, 0))

    return pl.pallas_call(
        attend_kernel,
        out_shape=jax.ShapeDtypeStruct((8, 2, HALF, 128), BF16),
        grid=(8 // CHUNK,),
        in_specs=[
            smem(),
            pl.BlockSpec((2, EMB, TOTAL), lambda t: (0, 0, 0)),
            pl.BlockSpec((2, TOTAL, EMB), lambda t: (0, 0, 0)),
            pl.BlockSpec((2, CHUNK, HALF, 128), lambda t: (0, t, 0, 0)),
            piece(4),
            piece(4),
            piece(4),
            piece(2),
            piece(2),
        ],
        out_specs=pl.BlockSpec((CHUNK, 2, HALF, 128), lambda t: (t, 0, 0, 0)),
        scratch_shapes=[pltpu.VMEM((CHUNK * HALF, TOTAL), F32) for _ in range(3)],
        compiler_params=params(),
        name="attend",
    )(at, k, v, q, *pieces)


def finish_kernel(
    at_ref, att_ref, gate_ref, x_ref, wf_ref, pinv_ref, g_ref, wl_ref, wr_ref, ac_ref, ar_ref, new_ref, left_ref, near_ref, far_ref
):
    gated = jnp.concatenate(
        [(gate_ref[h] * att_ref[h].astype(F32)).astype(BF16) for h in range(HEADS)], axis=1
    )
    gated = mm(pinv_ref[...], gated)
    w = jnp.concatenate([wf_ref[HEAD * (k // 4) : HEAD * (k // 4 + 1)] for k in range(4 * HEADS)], axis=0)
    slot = slot_of((ROWS, 4 * EMB))
    slot_one = slot_of((ROWS, 128))
    left = jnp.zeros((ROWS, 128), F32)
    for s in range(SEQS):
        inc = mm(jnp.where(slot == s, gated, 0.0).astype(BF16), w)
        new = (x_ref[s].astype(F32) + inc).astype(BF16)
        new_ref[s] = new
        n = normalised(new.astype(F32), g_ref[...])
        left = jnp.where(slot_one == s, mm(n, wl_ref[...]), left)
        right = mm_nt(wr_ref[...], n) * ar_ref[s : s + 1]
        rows = slice(HEAD * s, HEAD * (s + 1))
        halves = [right[:, :128], jnp.concatenate([right[:, COLS:], right[:, :32]], axis=1)]
        first = at_ref[1] == 0
        near_ref[rows] = jnp.where(first, halves[0], halves[1]).astype(BF16)
        far_ref[rows] = jnp.where(first, halves[1], halves[0]).astype(BF16)
    left = (left * ac_ref[...]).astype(BF16)
    for copy in range(PEERS_COL // 2):
        left_ref[copy] = left


def finish(*args):
    return pl.pallas_call(
        finish_kernel,
        out_shape=(
            jax.ShapeDtypeStruct((SEQS, ROWS, EMB), BF16),
            jax.ShapeDtypeStruct((PEERS_COL // 2, ROWS, 128), BF16),
            jax.ShapeDtypeStruct((128, 128), BF16),
            jax.ShapeDtypeStruct((128, 128), BF16),
        ),
        in_specs=[smem()] + [vmem()] * 10,
        compiler_params=params(),
        name="finish",
    )(*args)


STEP = 48


def outer_kernel(at_ref, lo_ref, lp_ref, r0, rp, rm, rt, w_ref, off_ref, ki_ref, kj_ref, z_ref, o_ref, l_all, r_all, lhs, rhs, obf):
    step = pl.program_id(0)

    @pl.when(step == 0)
    def _():
        core = at_ref[1]
        for p in range(PEERS_COL // 2):
            for side, ref in enumerate((lo_ref, lp_ref)):
                c = 2 * p + (core if side == 0 else 1 - core)
                l_all[pl.ds(pl.multiple_of(c * ROWS, ROWS), ROWS)] = ref[p].astype(F32)
        for d, ref in enumerate((r0, rp, rm, rt)):
            y = lax.rem(at_ref[2] + OFFSETS[d], 4)
            for e in range(2):
                zh = at_ref[3] if e == 0 else 1 - at_ref[3]
                for side in range(2):
                    c = 4 * y + 2 * zh + (core if side == 0 else 1 - core)
                    r_all[pl.ds(pl.multiple_of(c * 128, 128), 128)] = ref[e, side].astype(F32)
        for q in range(8):
            lines = [
                r_all[pl.ds(HEAD * s + 4 * q + b, PEERS_COL, stride=128), :] for b in range(4) for s in range(SEQS)
            ]
            turned = jnp.transpose(jnp.concatenate(lines, axis=0))
            lhs[COLS * q : COLS * (q + 1)] = turned[:COLS].astype(BF16)

    slot = slot_of((PEERS_COL, 128))
    for k in range(STEP):
        m = l_all[pl.ds(step * STEP + k, PEERS_COL, stride=ROWS), :]
        rolled = [m] + [pltpu.roll(m, HEAD * d, 1) for d in range(1, 4)]
        for b in range(4):
            for s in range(SEQS):
                at = 64 * b + 16 * s
                rhs[at : at + 16, 128 * k : 128 * (k + 1)] = jnp.where(slot == b, rolled[(b - s) % 4], 0.0).astype(BF16)
    for k in range(0, STEP, 2):
        outer = mm(lhs[...], rhs[:, 128 * k : 128 * (k + 2)]).astype(BF16)
        for e in range(2):
            for q in range(8):
                obf[COLS * (k + e) : COLS * (k + e + 1), 128 * q : 128 * (q + 1)] = outer[
                    COLS * q : COLS * (q + 1), 128 * e : 128 * (e + 1)
                ]
    update = mm(obf[...], w_ref[...]) + off_ref[...]
    for k in range(STEP):
        keep = kj_ref[...] * ki_ref[step * STEP + k]
        o_ref[k] = (z_ref[k].astype(F32) + update[COLS * k : COLS * (k + 1)] * keep).astype(BF16)


def outer_update(at, left_own, left_par, rights, w, offset, keep_i, keep_j, z):
    return pl.pallas_call(
        outer_kernel,
        out_shape=jax.ShapeDtypeStruct((ROWS, COLS, PAIR), BF16),
        grid=(ROWS // STEP,),
        in_specs=[
            smem(),
            pl.BlockSpec((PEERS_COL // 2, ROWS, 128), lambda t: (0, 0, 0)),
            pl.BlockSpec((PEERS_COL // 2, ROWS, 128), lambda t: (0, 0, 0)),
        ]
        + [pl.BlockSpec((2, 2, 128, 128), lambda t: (0, 0, 0, 0))] * 4
        + [
            pl.BlockSpec((1024, PAIR), lambda t: (0, 0)),
            pl.BlockSpec((1, PAIR), lambda t: (0, 0)),
            smem(),
            pl.BlockSpec((COLS, PAIR), lambda t: (0, 0)),
            pl.BlockSpec((STEP, COLS, PAIR), lambda t: (t, 0, 0)),
        ],
        out_specs=pl.BlockSpec((STEP, COLS, PAIR), lambda t: (t, 0, 0)),
        scratch_shapes=[
            pltpu.VMEM((PEERS_COL * ROWS, 128), F32),
            pltpu.VMEM((PEERS_COL * 128, 128), F32),
            pltpu.VMEM((8 * COLS, 256), BF16),
            pltpu.VMEM((256, 128 * STEP), BF16),
            pltpu.VMEM((STEP * COLS, 1024), BF16),
        ],
        compiler_params=params(),
        name="outer_update",
    )(at, left_own, left_par, *rights, w, offset, keep_i, keep_j, z)


def tables():
    expand = np.zeros((128, 4, 4, HEAD), np.float32)
    for u in range(4):
        for d in range(HEAD):
            expand[u * HEAD + d, u, :, d] = 1
    perm = np.zeros((ROWS, ROWS), np.float32)
    for i in range(ROWS):
        half, rest = divmod(i, HALF)
        perm[half * HALF + (rest % 4) * QUADS + rest // 4, i] = 1
    return expand.reshape(128, 512), perm


def swap_cores(x):
    return lax.ppermute(x, "core", [(0, 1), (1, 0)])


def along_y(x, d):
    return lax.ppermute(x, "y", [(a, (a + d) % 4) for a in range(4)])


def along_x(x, d):
    return lax.ppermute(x, "x", [(a, (a + d) % 4) for a in range(4)])


def swap_z(x):
    return lax.ppermute(x, "zl", [(0, 1), (1, 0)])


def turn_grid(x, cross):
    def index(a, b, c, d, k):
        return (((a * 2 + b) * 4 + c) * 2 + d) * 2 + k

    moves = [
        (index(a, b, c, d, k), index(c, d, a, b, k ^ cross))
        for a in range(4)
        for b in range(2)
        for c in range(4)
        for d in range(2)
        for k in range(2)
    ]
    return lax.ppermute(x, ROW + COL, moves)


def ring_pieces(block):
    up, down = along_y(block, 1), along_y(block, 3)
    return block, up, down, along_y(up[:, :2], 1), along_y(down[:, 2:], 3)


def on_device(
    alignment_embedding,
    couplings_embedding,
    alignment_availability,
    amino_availability,
    alignment_scaling_vector,
    attention_joint_matrix,
    attention_final_matrix,
    coupling_scaling_vector,
    coupling_logit_matrix,
    tensor_scaling_vector,
    first_factor_matrix,
    second_factor_matrix,
    tensor_projection_matrix,
    tensor_offset_vector,
):
    core = lax.axis_index("core")
    at = jnp.stack([lax.axis_index(name) for name in ("y", "core", "x", "zl")]).astype(jnp.int32)
    expand, perm = tables()

    bias = pair_bias(
        couplings_embedding.reshape(ROWS * COLS, PAIR),
        coupling_scaling_vector[None],
        jnp.repeat(coupling_logit_matrix.T, 16, axis=0),
    ).reshape(4 * HEADS, QUADS, 4 * COLS)
    bias = lax.all_to_all(bias, ROW + ("zh", "core"), 0, 0, tiled=True).reshape(8, 4, QUADS, 4 * COLS)

    present = alignment_availability.astype(BF16)
    sent_mask = jnp.pad(
        jnp.stack([present[:, :128], jnp.pad(present[:, 128:], ((0, 0), (0, 64)))]), ((0, 0), (0, 4), (0, 0))
    ).reshape(16, 128)
    own, gate = project(
        alignment_embedding,
        alignment_scaling_vector[None],
        attention_joint_matrix,
        jnp.asarray(expand, BF16),
        jnp.asarray(perm, BF16),
        sent_mask,
    )
    own, bias = lax.optimization_barrier((own, bias))
    own = lax.all_to_all(own, ROW, 0, 0, tiled=True)
    pieces = ring_pieces(bias)
    k, v, q = prepare(at, own, swap_cores(own))
    attended = attend(at, k, v, q, pieces).reshape(16, HALF, 128)
    attended = lax.all_to_all(attended, ROW + ("core",), 0, 0, tiled=True).reshape(HEADS, ROWS, 128)

    present = alignment_availability.astype(F32)
    alignment_refreshed, left, near, far = finish(
        at,
        attended,
        gate,
        alignment_embedding,
        attention_final_matrix,
        jnp.asarray(perm.T, BF16),
        tensor_scaling_vector[None],
        jnp.tile(first_factor_matrix, (1, 4)),
        second_factor_matrix.T,
        jnp.repeat(present.T, HEAD, axis=1),
        present,
    )
    left = lax.all_to_all(left, ("y", "zh"), 0, 0, tiled=True)
    right = jnp.stack([turn_grid(near, 0), turn_grid(far, 1)])
    right = jnp.stack([right, swap_z(right)])
    rights = [right] + [along_x(right, d) for d in (1, 3, 2)]

    keep = amino_availability.astype(F32)
    keep_i = lax.dynamic_slice_in_dim(keep, lax.axis_index(ROW) * ROWS, ROWS)
    keep_j = lax.dynamic_slice_in_dim(keep, lax.axis_index(COL) * COLS, COLS)
    projection = (tensor_projection_matrix.astype(F32) / 64).astype(BF16)
    projection = projection.reshape(HEAD, 8, 4, PAIR).transpose(1, 2, 0, 3).reshape(1024, PAIR)
    couplings_refreshed = outer_update(
        at,
        left,
        swap_cores(left),
        rights,
        projection,
        tensor_offset_vector[None],
        keep_i,
        jnp.broadcast_to(keep_j[:, None], (COLS, PAIR)),
        couplings_embedding,
    )
    return alignment_refreshed, couplings_refreshed


def solution(mesh):
    mesh = Mesh(mesh.devices.reshape(4, 2, 4, 2, 2), ROW + COL)
    placed = (P(COL, ROW, None), P(ROW, COL, None), P(COL, ROW)) + (P(),) * 11
    return jax.shard_map(
        on_device,
        mesh=mesh,
        in_specs=placed,
        out_specs=(P(COL, ROW, None), P(ROW, COL, None)),
        check_vma=False,
    )
```

```python
import jax
import jax.numpy as jnp
import numpy as np
from jax import lax
from jax.experimental import pallas as pl
from jax.experimental.pallas import tpu as pltpu
from jax.sharding import Mesh, PartitionSpec as P

F32 = jnp.float32
BF16 = jnp.bfloat16
HEADS = 8
HEAD = 32
SEQS = 4
ROWS = 192
HALF = 96
QUADS = 24
COLS = 96
EMB = 256
PAIR = 128
PEERS_COL = 16
TOTAL = 1536
CHUNK = 2
BIAS_AT = 48
Q_ROWS, K_ROWS, V_ROWS, M_ROWS = 0, 192, 384, 576
SENT_ROWS = 592
LOG2E = 1.4426950408889634
ROW = ("x", "zl")
COL = ("y", "zh", "core")


def mm(a, b):
    return jnp.dot(a, b, preferred_element_type=F32)


def mm_tn(a, b):
    return lax.dot_general(a, b, (((0,), (0,)), ((), ())), preferred_element_type=F32)


def normalised(x, gain):
    mean = jnp.mean(x, axis=-1, keepdims=True)
    d = x - mean
    var = jnp.mean(d * d, axis=-1, keepdims=True)
    return (d * lax.rsqrt(var + 1e-05) * gain).astype(BF16)


def slot_of(shape):
    return (lax.broadcasted_iota(jnp.int32, shape, len(shape) - 1) // HEAD) % 4


def params(mib):
    return pltpu.CompilerParams(vmem_limit_bytes=mib * 1024 * 1024)


def vmem():
    return pl.BlockSpec(memory_space=pltpu.VMEM)


def smem():
    return pl.BlockSpec(memory_space=pltpu.SMEM)


def project_kernel(x_ref, g_ref, w_ref, e_ref, p_ref, m_ref, qkv_ref, gate_ref):
    slot = slot_of((ROWS, 4 * 128))
    plain = [normalised(x_ref[s].astype(F32), g_ref[...]) for s in range(SEQS)]
    moved = [mm(p_ref[...], n).astype(BF16) for n in plain]
    for part in range(4):
        rows = moved if part in (0, 3) else plain
        for m in range(2):
            w = mm(w_ref[:, part * EMB + m * 128 : part * EMB + (m + 1) * 128], e_ref[...]).astype(BF16)
            acc = mm(rows[0], w)
            for s in range(1, SEQS):
                acc = jnp.where(slot == s, mm(rows[s], w), acc)
            for u in range(4):
                t = acc[:, u * 128 : (u + 1) * 128]
                h = 4 * m + u
                if part == 0:
                    qkv_ref[h, Q_ROWS:K_ROWS] = (t * HEAD ** (-0.5)).astype(BF16)
                elif part == 1:
                    qkv_ref[h, K_ROWS:V_ROWS] = t.astype(BF16)
                elif part == 2:
                    qkv_ref[h, V_ROWS:M_ROWS] = t.astype(BF16)
                else:
                    gate_ref[h] = jax.nn.sigmoid(t)
    for h in range(HEADS):
        qkv_ref[h, M_ROWS:] = m_ref[...]


def project(x, gain, w, expand, perm, present):
    return pl.pallas_call(
        project_kernel,
        out_shape=(
            jax.ShapeDtypeStruct((HEADS, SENT_ROWS, 128), BF16),
            jax.ShapeDtypeStruct((HEADS, ROWS, 128), F32),
        ),
        compiler_params=params(24),
        name="project",
    )(x, gain, w, expand, perm, present)


def bias_kernel(z_ref, g_ref, w_ref, o_ref):
    acc = jnp.zeros((4 * COLS, 128), F32)
    head = lax.broadcasted_iota(jnp.int32, (HEADS, 128), 0)
    lane = lax.broadcasted_iota(jnp.int32, (HEADS, 128), 1)
    w = mm_tn(w_ref[...], jnp.where(lane // 16 == head, 1.0, 0.0).astype(BF16))
    group = lax.broadcasted_iota(jnp.int32, (PAIR, 128), 1) % 16
    for k in range(8):
        n = normalised(z_ref[768 * k : 768 * (k + 1)].astype(F32), g_ref[...])
        both = jnp.concatenate([n[:384], n[384:]], axis=1)
        spread = [jnp.where(group == 2 * k + e, w, 0.0).astype(BF16) for e in range(2)]
        acc += mm(both, jnp.concatenate(spread, axis=0))
    out = jnp.transpose(acc).astype(BF16).reshape(HEADS, 16, 4 * COLS)
    for copy in range(2):
        o_ref[:, copy] = out


def pair_bias(z, gain, w):
    return pl.pallas_call(
        bias_kernel,
        out_shape=jax.ShapeDtypeStruct((HEADS, 2, 2 * QUADS, 4 * COLS), BF16),
        grid=(3,),
        in_specs=[
            pl.BlockSpec((6144, PAIR), lambda t: (t, 0)),
            pl.BlockSpec((1, PAIR), lambda t: (0, 0)),
            pl.BlockSpec((HEADS, PAIR), lambda t: (0, 0)),
        ],
        out_specs=pl.BlockSpec((HEADS, 2, 16, 4 * COLS), lambda t: (0, 0, t, 0)),
        compiler_params=params(60),
        name="pair_bias",
    )(z, gain, w)


OFFSETS = (0, 3, 1, 2)


def prepare_kernel(at_ref, own_ref, par_ref, k_ref, v_ref, q_ref):
    y = at_ref[0]
    core = at_ref[1]
    for side, ref in enumerate((own_ref, par_ref)):
        for d in range(4):
            first = 2 * lax.rem(y + OFFSETS[d], 4)
            span = slice(384 * d, 384 * (d + 1))
            keys = jnp.concatenate([ref[first + e, K_ROWS:V_ROWS] for e in range(2)], axis=0)
            k_ref[side, :128, span] = jnp.transpose(keys.astype(F32)).astype(BF16)
            for e in range(2):
                v_ref[side, 384 * d + ROWS * e : 384 * d + ROWS * (e + 1), :128] = ref[first + e, V_ROWS:M_ROWS]
            masks = [ref[first + e, M_ROWS:].astype(F32) for e in range(2)]
            line = jnp.concatenate([masks[0][:8], masks[0][8:, :64], masks[1][:8], masks[1][8:, :64]], axis=1)
            absent = (line - 1.0) * 1000000000.0
            rows = []
            for s in range(SEQS):
                rows += [absent[s : s + 1], jnp.zeros((15, 384), F32)]
            k_ref[side, 128:192, span] = jnp.concatenate(rows, axis=0).astype(BF16)
        v_ref[side, :, 128:] = jnp.ones((TOTAL, 128), BF16)
        for r in range(8):
            q_ref[side, r] = ref[r, pl.ds(pl.multiple_of(core * HALF, HALF), HALF)]


def prepare(at, own, par):
    return pl.pallas_call(
        prepare_kernel,
        out_shape=(
            jax.ShapeDtypeStruct((2, 192, TOTAL), BF16),
            jax.ShapeDtypeStruct((2, TOTAL, EMB), BF16),
            jax.ShapeDtypeStruct((2, 8, HALF, 128), BF16),
        ),
        in_specs=[smem(), vmem(), vmem()],
        out_specs=(vmem(), vmem(), vmem()),
        compiler_params=params(24),
        name="prepare",
    )(at, own, par)


def attend_kernel(at_ref, k_ref, v_ref, q_ref, b0, bp, bm, f1, f2, o_ref, rhs_even, rhs_odd, even, odd):
    core = at_ref[1]
    count = CHUNK * HALF
    for d, refs in enumerate(((b0,), (bp,), (bm,), (f1, f2))):
        for r in range(CHUNK):
            got = [ref[r, k].astype(F32) for ref in refs for k in range(4 // len(refs))]
            lines = [
                jnp.concatenate([g[:, COLS * u : COLS * (u + 1)] for g in got], axis=1) for u in range(4)
            ]
            block = jnp.concatenate(lines, axis=0).astype(BF16)
            for rhs in (rhs_even, rhs_odd):
                rhs[BIAS_AT + HALF * r : BIAS_AT + HALF * (r + 1), 384 * d : 384 * (d + 1)] = block
    for rhs in (rhs_even, rhs_odd):
        rhs[BIAS_AT + count :] = jnp.zeros((EMB - BIAS_AT - count, TOTAL), BF16)
    wide = slot_of((count, 256))
    lane = lax.broadcasted_iota(jnp.int32, (count, 256), 1)
    row = lax.broadcasted_iota(jnp.int32, (count, 256), 0)
    pick = jnp.where((lane == HEAD) | (lane == row + BIAS_AT), 1.0, 0.0)
    first = lane[:, :128] < HEAD
    tail = pick[:, 128:].astype(BF16)

    def scores(out, rhs, side, s):
        rhs[:HEAD] = k_ref[side, HEAD * s : HEAD * (s + 1)]
        rhs[HEAD:BIAS_AT] = k_ref[side, 128 + 16 * s : 128 + 16 * (s + 1)]
        q = jnp.concatenate([q_ref[side, r] for r in range(CHUNK)], axis=0).astype(F32)
        if s:
            q = pltpu.roll(q, 128 - HEAD * s, 1)
        lhs = jnp.concatenate([jnp.where(first, q, pick[:, :128]).astype(BF16), tail], axis=1)
        top = None
        for t in range(6):
            span = slice(256 * t, 256 * (t + 1))
            c = mm(lhs, rhs[:, span])
            out[:, span] = c
            both = jnp.maximum(c[:, :128], c[:, 128:])
            top = both if top is None else jnp.maximum(top, both)
        return jnp.max(top, axis=1, keepdims=True)

    def values(buf, top, side):
        e = jnp.exp(buf[...] - top).astype(BF16)
        return mm(e, v_ref[side])

    top = scores(even, rhs_even, 0, 0)
    for n in range(2 * SEQS):
        side, s = divmod(n, SEQS)
        now, later, rhs = (even, odd, rhs_odd) if n % 2 == 0 else (odd, even, rhs_even)
        if n < 2 * SEQS - 1:
            following = scores(later, rhs, *divmod(n + 1, SEQS))
        got = values(now, top, side)
        total = got if s == 0 else jnp.where(wide == s, got, total)
        if n < 2 * SEQS - 1:
            top = following
        if s == SEQS - 1:
            out = (total[:, :128] / total[:, 128:]).astype(BF16)
            quad = core if side == 0 else 1 - core
            for r in range(CHUNK):
                o_ref[r, quad] = out[HALF * r : HALF * (r + 1)]


def attend(at, k, v, q, pieces):
    def piece(parts):
        return pl.BlockSpec((CHUNK, parts, QUADS, 4 * COLS), lambda t: (t, 0, 0, 0))

    return pl.pallas_call(
        attend_kernel,
        out_shape=jax.ShapeDtypeStruct((8, 2, HALF, 128), BF16),
        grid=(8 // CHUNK,),
        in_specs=[
            smem(),
            pl.BlockSpec((2, 192, TOTAL), lambda t: (0, 0, 0)),
            pl.BlockSpec((2, TOTAL, EMB), lambda t: (0, 0, 0)),
            pl.BlockSpec((2, CHUNK, HALF, 128), lambda t: (0, t, 0, 0)),
            piece(4),
            piece(4),
            piece(4),
            piece(2),
            piece(2),
        ],
        out_specs=pl.BlockSpec((CHUNK, 2, HALF, 128), lambda t: (t, 0, 0, 0)),
        scratch_shapes=[pltpu.VMEM((EMB, TOTAL), BF16)] * 2 + [pltpu.VMEM((CHUNK * HALF, TOTAL), F32)] * 2,
        compiler_params=params(28),
        name="attend",
    )(at, k, v, q, *pieces)


def finish_kernel(
    at_ref, att_ref, gate_ref, x_ref, wf_ref, pinv_ref, g_ref, wl_ref, wr_ref, ac_ref, new_ref, left_ref, near_ref, far_ref
):
    gated = jnp.concatenate(
        [(gate_ref[h] * att_ref[h].astype(F32)).astype(BF16) for h in range(HEADS)], axis=1
    )
    gated = mm(pinv_ref[...], gated)
    w = jnp.concatenate([wf_ref[HEAD * (k // 4) : HEAD * (k // 4 + 1)] for k in range(4 * HEADS)], axis=0)
    slot = slot_of((ROWS, 4 * EMB))
    slot_one = slot_of((ROWS, 128))
    left = jnp.zeros((ROWS, 128), F32)
    right = jnp.zeros((ROWS, 128), F32)
    for s in range(SEQS):
        inc = mm(jnp.where(slot == s, gated, 0.0).astype(BF16), w)
        new = (x_ref[s].astype(F32) + inc).astype(BF16)
        new_ref[s] = new
        n = normalised(new.astype(F32), g_ref[...])
        left = jnp.where(slot_one == s, mm(n, wl_ref[...]), left)
        right = jnp.where(slot_one == s, mm(n, wr_ref[...]), right)
    right = right * ac_ref[...]
    first = at_ref[1] == 0
    near_ref[...] = jnp.where(first, right[:HALF], right[HALF:]).astype(BF16)
    far_ref[...] = jnp.where(first, right[HALF:], right[:HALF]).astype(BF16)
    left = (left * ac_ref[...]).astype(BF16)
    for copy in range(PEERS_COL // 2):
        left_ref[copy] = left


def finish(*args):
    return pl.pallas_call(
        finish_kernel,
        out_shape=(
            jax.ShapeDtypeStruct((SEQS, ROWS, EMB), BF16),
            jax.ShapeDtypeStruct((PEERS_COL // 2, ROWS, 128), BF16),
            jax.ShapeDtypeStruct((HALF, 128), BF16),
            jax.ShapeDtypeStruct((HALF, 128), BF16),
        ),
        in_specs=[smem()] + [vmem()] * 9,
        compiler_params=params(24),
        name="finish",
    )(*args)


STEP = 48


def columns_kernel(at_ref, r_ref, o_ref, r_all):
    core = at_ref[1]
    pad = jnp.zeros((128 - COLS, 128), F32)
    for p in range(PEERS_COL // 2):
        for side in range(2):
            c = 2 * p + (core if side == 0 else 1 - core)
            turned = jnp.transpose(jnp.concatenate([r_ref[p, side].astype(F32), pad], axis=0))
            r_all[pl.ds(pl.multiple_of(c * 128, 128), 128)] = turned
    for q in range(8):
        lines = [
            r_all[pl.ds(HEAD * s + 4 * q + b, PEERS_COL, stride=128), :] for b in range(4) for s in range(SEQS)
        ]
        turned = jnp.transpose(jnp.concatenate(lines, axis=0))
        o_ref[COLS * q : COLS * (q + 1)] = turned[:COLS].astype(BF16)


def columns(at, right):
    return pl.pallas_call(
        columns_kernel,
        out_shape=jax.ShapeDtypeStruct((8 * COLS, EMB), BF16),
        in_specs=[smem(), vmem()],
        out_specs=vmem(),
        scratch_shapes=[pltpu.VMEM((PEERS_COL * 128, 128), F32)],
        compiler_params=params(16),
        name="columns",
    )(at, right)


def outer_kernel(at_ref, lo_ref, lp_ref, lhs, w_ref, off_ref, ki_ref, kj_ref, z_ref, o_ref, l_all, rhs, obf):
    step = pl.program_id(0)

    @pl.when(step == 0)
    def _():
        core = at_ref[1]
        for p in range(PEERS_COL // 2):
            for side, ref in enumerate((lo_ref, lp_ref)):
                c = 2 * p + (core if side == 0 else 1 - core)
                l_all[pl.ds(pl.multiple_of(c * ROWS, ROWS), ROWS)] = ref[p].astype(F32)

    slot = slot_of((PEERS_COL, 128))
    for k in range(STEP):
        m = l_all[pl.ds(step * STEP + k, PEERS_COL, stride=ROWS), :]
        rolled = [m] + [pltpu.roll(m, HEAD * d, 1) for d in range(1, 4)]
        for b in range(4):
            for s in range(SEQS):
                at = 64 * b + 16 * s
                rhs[at : at + 16, 128 * k : 128 * (k + 1)] = jnp.where(slot == b, rolled[(b - s) % 4], 0.0).astype(BF16)
    for k in range(0, STEP, 2):
        outer = mm(lhs[...], rhs[:, 128 * k : 128 * (k + 2)]).astype(BF16)
        for e in range(2):
            for q in range(8):
                obf[COLS * (k + e) : COLS * (k + e + 1), 128 * q : 128 * (q + 1)] = outer[
                    COLS * q : COLS * (q + 1), 128 * e : 128 * (e + 1)
                ]
    update = mm(obf[...], w_ref[...]) + off_ref[...]
    for k in range(STEP):
        keep = kj_ref[...] * ki_ref[step * STEP + k]
        o_ref[k] = (z_ref[k].astype(F32) + update[COLS * k : COLS * (k + 1)] * keep).astype(BF16)


def outer_update(at, left_own, left_par, right, w, offset, keep_i, keep_j, z):
    return pl.pallas_call(
        outer_kernel,
        out_shape=jax.ShapeDtypeStruct((ROWS, COLS, PAIR), BF16),
        grid=(ROWS // STEP,),
        in_specs=[
            smem(),
            pl.BlockSpec((PEERS_COL // 2, ROWS, 128), lambda t: (0, 0, 0)),
            pl.BlockSpec((PEERS_COL // 2, ROWS, 128), lambda t: (0, 0, 0)),
            pl.BlockSpec((8 * COLS, EMB), lambda t: (0, 0)),
            pl.BlockSpec((1024, PAIR), lambda t: (0, 0)),
            pl.BlockSpec((1, PAIR), lambda t: (0, 0)),
            smem(),
            pl.BlockSpec((COLS, PAIR), lambda t: (0, 0)),
            pl.BlockSpec((STEP, COLS, PAIR), lambda t: (t, 0, 0)),
        ],
        out_specs=pl.BlockSpec((STEP, COLS, PAIR), lambda t: (t, 0, 0)),
        scratch_shapes=[
            pltpu.VMEM((PEERS_COL * ROWS, 128), F32),
            pltpu.VMEM((256, 128 * STEP), BF16),
            pltpu.VMEM((STEP * COLS, 1024), BF16),
        ],
        compiler_params=params(60),
        name="outer_update",
    )(at, left_own, left_par, right, w, offset, keep_i, keep_j, z)


def tables():
    expand = np.zeros((128, 4, 4, HEAD), np.float32)
    for u in range(4):
        for d in range(HEAD):
            expand[u * HEAD + d, u, :, d] = 1
    perm = np.zeros((ROWS, ROWS), np.float32)
    for i in range(ROWS):
        half, rest = divmod(i, HALF)
        perm[half * HALF + (rest % 4) * QUADS + rest // 4, i] = 1
    return expand.reshape(128, 512), perm


def swap_cores(x):
    return lax.ppermute(x, "core", [(0, 1), (1, 0)])


def along_y(x, d):
    return lax.ppermute(x, "y", [(a, (a + d) % 4) for a in range(4)])


def turn_grid(x, cross):
    def index(a, b, c, d, k):
        return (((a * 2 + b) * 4 + c) * 2 + d) * 2 + k

    moves = [
        (index(a, b, c, d, k), index(c, d, a, b, k ^ cross))
        for a in range(4)
        for b in range(2)
        for c in range(4)
        for d in range(2)
        for k in range(2)
    ]
    return lax.ppermute(x, ROW + COL, moves)


def to_all(x, axes, n):
    return lax.all_to_all(jnp.broadcast_to(x[None], (n,) + x.shape), axes, 0, 0, tiled=True)


def on_device(
    alignment_embedding,
    couplings_embedding,
    alignment_availability,
    amino_availability,
    alignment_scaling_vector,
    attention_joint_matrix,
    attention_final_matrix,
    coupling_scaling_vector,
    coupling_logit_matrix,
    tensor_scaling_vector,
    first_factor_matrix,
    second_factor_matrix,
    tensor_projection_matrix,
    tensor_offset_vector,
):
    core = lax.axis_index("core")
    at = jnp.stack([lax.axis_index(name) for name in ("y", "core")]).astype(jnp.int32)
    expand, perm = tables()

    bias = pair_bias(
        couplings_embedding.reshape(ROWS * COLS, PAIR),
        coupling_scaling_vector[None],
        coupling_logit_matrix.T,
    ).reshape(4 * HEADS, QUADS, 4 * COLS)
    bias = lax.all_to_all(bias, ROW + ("zh", "core"), 0, 0, tiled=True).reshape(8, 4, QUADS, 4 * COLS)

    keep = amino_availability.astype(F32)
    keep_i = lax.dynamic_slice_in_dim(keep, lax.axis_index(ROW) * ROWS, ROWS)
    keep_j = lax.dynamic_slice_in_dim(keep, lax.axis_index(COL) * COLS, COLS)
    keep_j = jnp.broadcast_to(keep_j[:, None], (COLS, PAIR))
    present = alignment_availability.astype(BF16)
    sent_mask = jnp.pad(
        jnp.stack([present[:, :128], jnp.pad(present[:, 128:], ((0, 0), (0, 64)))]), ((0, 0), (0, 4), (0, 0))
    ).reshape(16, 128)
    own, gate = project(
        alignment_embedding,
        alignment_scaling_vector[None],
        attention_joint_matrix,
        jnp.asarray(expand, BF16),
        jnp.asarray(perm, BF16),
        sent_mask,
    )
    own, bias, at, keep_i, keep_j = lax.optimization_barrier((own, bias, at, keep_i, keep_j))
    up, down = along_y(bias, 1), along_y(bias, 3)
    own = lax.all_to_all(own, ROW, 0, 0, tiled=True)
    own = lax.optimization_barrier((own, up, down))[0]
    pieces = (bias, up, down, along_y(up[:, :2], 1), along_y(down[:, 2:], 3))
    k, v, q = prepare(at, own, swap_cores(own))
    attended = attend(at, k, v, q, pieces).reshape(16, HALF, 128)
    attended = lax.all_to_all(attended, ROW + ("core",), 0, 0, tiled=True).reshape(HEADS, ROWS, 128)

    present = alignment_availability.astype(F32)
    alignment_refreshed, left, near, far = finish(
        at,
        attended,
        gate,
        alignment_embedding,
        attention_final_matrix,
        jnp.asarray(perm.T, BF16),
        tensor_scaling_vector[None],
        jnp.tile(first_factor_matrix, (1, 4)),
        jnp.tile(second_factor_matrix, (1, 4)),
        jnp.repeat(present.T, HEAD, axis=1),
    )
    left = lax.all_to_all(left, ("y", "zh"), 0, 0, tiled=True)
    right = jnp.stack([turn_grid(near, 0), turn_grid(far, 1)])
    right = columns(at, to_all(right, ROW, 8))

    projection = (tensor_projection_matrix.astype(F32) / 64).astype(BF16)
    projection = projection.reshape(HEAD, 8, 4, PAIR).transpose(1, 2, 0, 3).reshape(1024, PAIR)
    couplings_refreshed = outer_update(
        at,
        left,
        swap_cores(left),
        right,
        projection,
        tensor_offset_vector[None],
        keep_i,
        keep_j,
        couplings_embedding,
    )
    return alignment_refreshed, couplings_refreshed


def solution(mesh):
    mesh = Mesh(mesh.devices.reshape(4, 2, 4, 2, 2), ROW + COL)
    placed = (P(COL, ROW, None), P(ROW, COL, None), P(COL, ROW)) + (P(),) * 11
    return jax.shard_map(
        on_device,
        mesh=mesh,
        in_specs=placed,
        out_specs=(P(COL, ROW, None), P(ROW, COL, None)),
        check_vma=False,
    )
```

```python
import jax
import jax.numpy as jnp
import numpy as np
from jax import lax
from jax.experimental import pallas as pl
from jax.experimental.pallas import tpu as pltpu
from jax.sharding import Mesh, PartitionSpec as P

F32 = jnp.float32
BF16 = jnp.bfloat16
HEADS = 8
HEAD = 32
SEQS = 4
ROWS = 192
HALF = 96
QUADS = 24
COLS = 96
EMB = 256
PAIR = 128
PEERS_COL = 16
TOTAL = 1536
CHUNK = 2
BIAS_AT = 48
EARLY = 1152
Q_ROWS, K_ROWS, V_ROWS, M_ROWS = 0, 192, 384, 576
SENT_ROWS = 592
LOG2E = 1.4426950408889634
ROW = ("x", "zl")
COL = ("y", "zh", "core")


def mm(a, b):
    return jnp.dot(a, b, preferred_element_type=F32)


def mm_tn(a, b):
    return lax.dot_general(a, b, (((0,), (0,)), ((), ())), preferred_element_type=F32)


def normalised(x, gain):
    mean = jnp.mean(x, axis=-1, keepdims=True)
    d = x - mean
    var = jnp.mean(d * d, axis=-1, keepdims=True)
    return (d * lax.rsqrt(var + 1e-05) * gain).astype(BF16)


def slot_of(shape):
    return (lax.broadcasted_iota(jnp.int32, shape, len(shape) - 1) // HEAD) % 4


def params(mib):
    return pltpu.CompilerParams(vmem_limit_bytes=mib * 1024 * 1024)


def vmem():
    return pl.BlockSpec(memory_space=pltpu.VMEM)


def smem():
    return pl.BlockSpec(memory_space=pltpu.SMEM)


def project_kernel(x_ref, g_ref, w_ref, e_ref, p_ref, m_ref, keep_ref, qkv_ref, gate_ref, column_ref):
    slot = slot_of((ROWS, 4 * 128))
    plain = [normalised(x_ref[s].astype(F32), g_ref[...]) for s in range(SEQS)]
    moved = [mm(p_ref[...], n).astype(BF16) for n in plain]
    for part in range(4):
        rows = moved if part in (0, 3) else plain
        for m in range(2):
            w = mm(w_ref[:, part * EMB + m * 128 : part * EMB + (m + 1) * 128], e_ref[...]).astype(BF16)
            acc = mm(rows[0], w)
            for s in range(1, SEQS):
                acc = jnp.where(slot == s, mm(rows[s], w), acc)
            for u in range(4):
                t = acc[:, u * 128 : (u + 1) * 128]
                h = 4 * m + u
                if part == 0:
                    qkv_ref[h, Q_ROWS:K_ROWS] = (t * HEAD ** (-0.5)).astype(BF16)
                elif part == 1:
                    qkv_ref[h, K_ROWS:V_ROWS] = t.astype(BF16)
                elif part == 2:
                    qkv_ref[h, V_ROWS:M_ROWS] = t.astype(BF16)
                else:
                    gate_ref[h] = jax.nn.sigmoid(t)
    for h in range(HEADS):
        qkv_ref[h, M_ROWS:] = m_ref[...]
    column_ref[...] = jnp.transpose(jnp.broadcast_to(keep_ref[...], (128, 128)))[:COLS]


def project(x, gain, w, expand, perm, present, keep):
    return pl.pallas_call(
        project_kernel,
        out_shape=(
            jax.ShapeDtypeStruct((HEADS, SENT_ROWS, 128), BF16),
            jax.ShapeDtypeStruct((HEADS, ROWS, 128), F32),
            jax.ShapeDtypeStruct((COLS, 128), F32),
        ),
        compiler_params=params(24),
        name="project",
    )(x, gain, w, expand, perm, present, keep)


def bias_kernel(z_ref, g_ref, w_ref, o_ref):
    acc = jnp.zeros((4 * COLS, 128), F32)
    head = lax.broadcasted_iota(jnp.int32, (HEADS, 128), 0)
    lane = lax.broadcasted_iota(jnp.int32, (HEADS, 128), 1)
    w = mm_tn(w_ref[...], jnp.where(lane // 16 == head, 1.0, 0.0).astype(BF16))
    group = lax.broadcasted_iota(jnp.int32, (PAIR, 128), 1) % 16
    for k in range(8):
        n = normalised(z_ref[768 * k : 768 * (k + 1)].astype(F32), g_ref[...])
        both = jnp.concatenate([n[:384], n[384:]], axis=1)
        spread = [jnp.where(group == 2 * k + e, w, 0.0).astype(BF16) for e in range(2)]
        acc += mm(both, jnp.concatenate(spread, axis=0))
    out = jnp.transpose(acc).astype(BF16).reshape(HEADS, 16, 4 * COLS)
    for copy in range(2):
        o_ref[:, copy] = out


def pair_bias(z, gain, w):
    return pl.pallas_call(
        bias_kernel,
        out_shape=jax.ShapeDtypeStruct((HEADS, 2, 2 * QUADS, 4 * COLS), BF16),
        grid=(3,),
        in_specs=[
            pl.BlockSpec((6144, PAIR), lambda t: (t, 0)),
            pl.BlockSpec((1, PAIR), lambda t: (0, 0)),
            pl.BlockSpec((HEADS, PAIR), lambda t: (0, 0)),
        ],
        out_specs=pl.BlockSpec((HEADS, 2, 16, 4 * COLS), lambda t: (0, 0, t, 0)),
        compiler_params=params(60),
        name="pair_bias",
    )(z, gain, w)


OFFSETS = (0, 3, 1, 2)


def prepare_kernel(at_ref, own_ref, par_ref, k_ref, v_ref, q_ref):
    y = at_ref[0]
    core = at_ref[1]
    for side, ref in enumerate((own_ref, par_ref)):
        for d in range(4):
            first = 2 * lax.rem(y + OFFSETS[d], 4)
            span = slice(384 * d, 384 * (d + 1))
            keys = jnp.concatenate([ref[first + e, K_ROWS:V_ROWS] for e in range(2)], axis=0)
            k_ref[side, :128, span] = jnp.transpose(keys.astype(F32)).astype(BF16)
            for e in range(2):
                v_ref[side, 384 * d + ROWS * e : 384 * d + ROWS * (e + 1), :128] = ref[first + e, V_ROWS:M_ROWS]
            masks = [ref[first + e, M_ROWS:].astype(F32) for e in range(2)]
            line = jnp.concatenate([masks[0][:8], masks[0][8:, :64], masks[1][:8], masks[1][8:, :64]], axis=1)
            absent = (line - 1.0) * 1000000000.0
            rows = []
            for s in range(SEQS):
                rows += [absent[s : s + 1], jnp.zeros((15, 384), F32)]
            k_ref[side, 128:192, span] = jnp.concatenate(rows, axis=0).astype(BF16)
        v_ref[side, :, 128:] = jnp.ones((TOTAL, 128), BF16)
        for r in range(8):
            q_ref[side, r] = ref[r, pl.ds(pl.multiple_of(core * HALF, HALF), HALF)]


def prepare(at, own, par):
    return pl.pallas_call(
        prepare_kernel,
        out_shape=(
            jax.ShapeDtypeStruct((2, 192, TOTAL), BF16),
            jax.ShapeDtypeStruct((2, TOTAL, EMB), BF16),
            jax.ShapeDtypeStruct((2, 8, HALF, 128), BF16),
        ),
        in_specs=[smem(), vmem(), vmem()],
        out_specs=(vmem(), vmem(), vmem()),
        compiler_params=params(24),
        name="prepare",
    )(at, own, par)


def attend_setup(pieces, rhs_pair, width):
    count = CHUNK * HALF
    for d, refs in enumerate(pieces):
        for r in range(CHUNK):
            got = [ref[r, k].astype(F32) for ref in refs for k in range(4 // len(refs))]
            lines = [
                jnp.concatenate([g[:, COLS * u : COLS * (u + 1)] for g in got], axis=1) for u in range(4)
            ]
            block = jnp.concatenate(lines, axis=0).astype(BF16)
            for rhs in rhs_pair:
                rhs[BIAS_AT + HALF * r : BIAS_AT + HALF * (r + 1), 384 * d : 384 * (d + 1)] = block
    for rhs in rhs_pair:
        rhs[BIAS_AT + count :] = jnp.zeros((EMB - BIAS_AT - count, width), BF16)


def attend_scores(k_ref, q_ref, width):
    count = CHUNK * HALF
    lane = lax.broadcasted_iota(jnp.int32, (count, 256), 1)
    row = lax.broadcasted_iota(jnp.int32, (count, 256), 0)
    pick = jnp.where((lane == HEAD) | (lane == row + BIAS_AT), 1.0, 0.0)
    first = lane[:, :128] < HEAD
    tail = pick[:, 128:].astype(BF16)

    def scores(out, rhs, side, s):
        rhs[:HEAD] = k_ref[side, HEAD * s : HEAD * (s + 1)]
        rhs[HEAD:BIAS_AT] = k_ref[side, 128 + 16 * s : 128 + 16 * (s + 1)]
        q = jnp.concatenate([q_ref[side, r] for r in range(CHUNK)], axis=0).astype(F32)
        if s:
            q = pltpu.roll(q, 128 - HEAD * s, 1)
        lhs = jnp.concatenate([jnp.where(first, q, pick[:, :128]).astype(BF16), tail], axis=1)
        top = None
        for at in range(0, width, 256):
            span = slice(at, min(at + 256, width))
            c = mm(lhs, rhs[:, span])
            out[:, span] = c
            for half in range(0, c.shape[1], 128):
                part = c[:, half : half + 128]
                top = part if top is None else jnp.maximum(top, part)
        return jnp.max(top, axis=1, keepdims=True)

    return scores


def attend_first_kernel(k_ref, v_ref, q_ref, b0, bp, bm, sum_ref, top_ref, rhs_even, rhs_odd, even, odd):
    count = CHUNK * HALF
    attend_setup(((b0,), (bp,), (bm,)), (rhs_even, rhs_odd), EARLY)
    scores = attend_scores(k_ref, q_ref, EARLY)
    wide = slot_of((count, 256))
    top = scores(even, rhs_even, 0, 0)
    for n in range(2 * SEQS):
        side, s = divmod(n, SEQS)
        now, later, rhs = (even, odd, rhs_odd) if n % 2 == 0 else (odd, even, rhs_even)
        if n < 2 * SEQS - 1:
            following = scores(later, rhs, *divmod(n + 1, SEQS))
        got = mm(jnp.exp(now[...] - top).astype(BF16), v_ref[side])
        total = got if s == 0 else jnp.where(wide == s, got, total)
        top_ref[side, s] = jnp.broadcast_to(top, (count, 128))
        if n < 2 * SEQS - 1:
            top = following
        if s == SEQS - 1:
            sum_ref[side] = total


def attend_last_kernel(at_ref, k_ref, v_ref, q_ref, f1, f2, sum_ref, top_ref, o_ref, rhs_all, buf_all):
    core = at_ref[1]
    count = CHUNK * HALF
    late = TOTAL - EARLY
    attend_setup(((f1, f2),), [rhs_all.at[n] for n in range(2 * SEQS)], late)
    scores = attend_scores(k_ref, q_ref, late)
    wide = slot_of((count, 256))
    peaks = [scores(buf_all.at[n], rhs_all.at[n], *divmod(n, SEQS)) for n in range(2 * SEQS)]
    for n in range(2 * SEQS):
        side, s = divmod(n, SEQS)
        before = top_ref[side, s]
        peak = jnp.maximum(peaks[n], before)
        e = jnp.exp(buf_all[n] - jnp.concatenate([peak] * (late // 128), axis=1)).astype(BF16)
        shrink = jnp.exp(before - peak)
        got = mm(e, v_ref[side]) + sum_ref[side] * jnp.concatenate([shrink, shrink], axis=1)
        total = got if s == 0 else jnp.where(wide == s, got, total)
        if s == SEQS - 1:
            out = (total[:, :128] / total[:, 128:]).astype(BF16)
            quad = core if side == 0 else 1 - core
            for r in range(CHUNK):
                o_ref[r, quad] = out[HALF * r : HALF * (r + 1)]


def attend(at, k, v, q, pieces):
    count = CHUNK * HALF
    late = TOTAL - EARLY

    def piece(parts):
        return pl.BlockSpec((CHUNK, parts, QUADS, 4 * COLS), lambda t: (t, 0, 0, 0))

    def scratch(width):
        return [pltpu.VMEM((EMB, width), BF16)] * 2 + [pltpu.VMEM((count, width), F32)] * 2

    queries = pl.BlockSpec((2, CHUNK, HALF, 128), lambda t: (0, t, 0, 0))
    sums = pl.BlockSpec((2, count, 256), lambda t: (0, t, 0))
    tops = pl.BlockSpec((2, SEQS, count, 128), lambda t: (0, 0, t, 0))
    total, top = pl.pallas_call(
        attend_first_kernel,
        out_shape=(
            jax.ShapeDtypeStruct((2, 8 * HALF, 256), F32),
            jax.ShapeDtypeStruct((2, SEQS, 8 * HALF, 128), F32),
        ),
        grid=(8 // CHUNK,),
        in_specs=[
            pl.BlockSpec((2, 192, EARLY), lambda t: (0, 0, 0)),
            pl.BlockSpec((2, EARLY, EMB), lambda t: (0, 0, 0)),
            queries,
            piece(4),
            piece(4),
            piece(4),
        ],
        out_specs=(sums, tops),
        scratch_shapes=scratch(EARLY),
        compiler_params=params(28),
        name="attend_first",
    )(k, v, q, *pieces[:3])
    return pl.pallas_call(
        attend_last_kernel,
        out_shape=jax.ShapeDtypeStruct((8, 2, HALF, 128), BF16),
        grid=(8 // CHUNK,),
        in_specs=[
            smem(),
            pl.BlockSpec((2, 192, late), lambda t: (0, 0, EARLY // late)),
            pl.BlockSpec((2, late, EMB), lambda t: (0, EARLY // late, 0)),
            queries,
            piece(2),
            piece(2),
            sums,
            tops,
        ],
        out_specs=pl.BlockSpec((CHUNK, 2, HALF, 128), lambda t: (t, 0, 0, 0)),
        scratch_shapes=[pltpu.VMEM((2 * SEQS, EMB, late), BF16), pltpu.VMEM((2 * SEQS, count, late), F32)],
        compiler_params=params(28),
        name="attend_last",
    )(at, k, v, q, *pieces[3:], total, top)


def finish_kernel(
    at_ref, att_ref, gate_ref, x_ref, wf_ref, pinv_ref, g_ref, wl_ref, wr_ref, ac_ref, new_ref, left_ref, near_ref, far_ref
):
    gated = jnp.concatenate(
        [(gate_ref[h] * att_ref[h].astype(F32)).astype(BF16) for h in range(HEADS)], axis=1
    )
    gated = mm(pinv_ref[...], gated)
    w = jnp.concatenate([wf_ref[HEAD * (k // 4) : HEAD * (k // 4 + 1)] for k in range(4 * HEADS)], axis=0)
    slot = slot_of((ROWS, 4 * EMB))
    slot_one = slot_of((ROWS, 128))
    left = jnp.zeros((ROWS, 128), F32)
    right = jnp.zeros((ROWS, 128), F32)
    for s in range(SEQS):
        inc = mm(jnp.where(slot == s, gated, 0.0).astype(BF16), w)
        new = (x_ref[s].astype(F32) + inc).astype(BF16)
        new_ref[s] = new
        n = normalised(new.astype(F32), g_ref[...])
        left = jnp.where(slot_one == s, mm(n, wl_ref[...]), left)
        right = jnp.where(slot_one == s, mm(n, wr_ref[...]), right)
    right = right * ac_ref[...]
    first = at_ref[1] == 0
    near_ref[...] = jnp.where(first, right[:HALF], right[HALF:]).astype(BF16)
    far_ref[...] = jnp.where(first, right[HALF:], right[:HALF]).astype(BF16)
    left = (left * ac_ref[...]).astype(BF16)
    for copy in range(PEERS_COL // 2):
        left_ref[copy] = left


def finish(*args):
    return pl.pallas_call(
        finish_kernel,
        out_shape=(
            jax.ShapeDtypeStruct((SEQS, ROWS, EMB), BF16),
            jax.ShapeDtypeStruct((PEERS_COL // 2, ROWS, 128), BF16),
            jax.ShapeDtypeStruct((HALF, 128), BF16),
            jax.ShapeDtypeStruct((HALF, 128), BF16),
        ),
        in_specs=[smem()] + [vmem()] * 9,
        compiler_params=params(24),
        name="finish",
    )(*args)


STEP = 64
PART = 16


def outer_kernel(at_ref, lo_ref, lp_ref, r_ref, w_ref, off_ref, ki_ref, kj_ref, z_ref, o_ref, l_all, r_all, lhs, rhs, *obf):
    step = pl.program_id(0)

    @pl.when(step == 0)
    def _():
        core = at_ref[1]
        pad = jnp.zeros((128 - COLS, 128), F32)
        for p in range(PEERS_COL // 2):
            for side, ref in enumerate((lo_ref, lp_ref)):
                c = 2 * p + (core if side == 0 else 1 - core)
                l_all[pl.ds(pl.multiple_of(c * ROWS, ROWS), ROWS)] = ref[p].astype(F32)
                turned = jnp.transpose(jnp.concatenate([r_ref[p, side].astype(F32), pad], axis=0))
                r_all[pl.ds(pl.multiple_of(c * 128, 128), 128)] = turned
        for q in range(8):
            lines = [
                r_all[pl.ds(HEAD * s + 4 * q + b, PEERS_COL, stride=128), :] for b in range(4) for s in range(SEQS)
            ]
            turned = jnp.transpose(jnp.concatenate(lines, axis=0))
            lhs[COLS * q : COLS * (q + 1)] = turned[:COLS].astype(BF16)

    slot = slot_of((PEERS_COL, 128))
    for k in range(STEP):
        m = l_all[pl.ds(step * STEP + k, PEERS_COL, stride=ROWS), :]
        rolled = [m] + [pltpu.roll(m, HEAD * d, 1) for d in range(1, 4)]
        for b in range(4):
            for s in range(SEQS):
                at = 64 * b + 16 * s
                rhs[at : at + 16, 128 * k : 128 * (k + 1)] = jnp.where(slot == b, rolled[(b - s) % 4], 0.0).astype(BF16)

    def products(part):
        for k in range(0, PART, 2):
            at = 128 * (PART * part + k)
            outer = mm(lhs[...], rhs[:, at : at + 256]).astype(BF16)
            for e in range(2):
                for q in range(8):
                    obf[part % 2][COLS * (k + e) : COLS * (k + e + 1), 128 * q : 128 * (q + 1)] = outer[
                        COLS * q : COLS * (q + 1), 128 * e : 128 * (e + 1)
                    ]

    def project_part(part):
        update = mm(obf[part % 2][...], w_ref[...]) + off_ref[...]
        for k in range(PART):
            i = PART * part + k
            keep = kj_ref[...] * ki_ref[step * STEP + i]
            o_ref[i] = (z_ref[i].astype(F32) + update[COLS * k : COLS * (k + 1)] * keep).astype(BF16)

    products(0)
    for part in range(1, STEP // PART):
        products(part)
        project_part(part - 1)
    project_part(STEP // PART - 1)


def outer_update(at, left_own, left_par, right, w, offset, keep_i, keep_j, z):
    return pl.pallas_call(
        outer_kernel,
        out_shape=jax.ShapeDtypeStruct((ROWS, COLS, PAIR), BF16),
        grid=(ROWS // STEP,),
        in_specs=[
            smem(),
            pl.BlockSpec((PEERS_COL // 2, ROWS, 128), lambda t: (0, 0, 0)),
            pl.BlockSpec((PEERS_COL // 2, ROWS, 128), lambda t: (0, 0, 0)),
            pl.BlockSpec((PEERS_COL // 2, 2, COLS, 128), lambda t: (0, 0, 0, 0)),
            pl.BlockSpec((1024, PAIR), lambda t: (0, 0)),
            pl.BlockSpec((1, PAIR), lambda t: (0, 0)),
            smem(),
            pl.BlockSpec((COLS, PAIR), lambda t: (0, 0)),
            pl.BlockSpec((STEP, COLS, PAIR), lambda t: (t, 0, 0)),
        ],
        out_specs=pl.BlockSpec((STEP, COLS, PAIR), lambda t: (t, 0, 0)),
        scratch_shapes=[
            pltpu.VMEM((PEERS_COL * ROWS, 128), F32),
            pltpu.VMEM((PEERS_COL * 128, 128), F32),
            pltpu.VMEM((8 * COLS, EMB), BF16),
            pltpu.VMEM((256, 128 * STEP), BF16),
            pltpu.VMEM((PART * COLS, 1024), BF16),
            pltpu.VMEM((PART * COLS, 1024), BF16),
        ],
        compiler_params=params(63),
        name="outer_update",
    )(at, left_own, left_par, right, w, offset, keep_i, keep_j, z)


def tables():
    expand = np.zeros((128, 4, 4, HEAD), np.float32)
    for u in range(4):
        for d in range(HEAD):
            expand[u * HEAD + d, u, :, d] = 1
    perm = np.zeros((ROWS, ROWS), np.float32)
    for i in range(ROWS):
        half, rest = divmod(i, HALF)
        perm[half * HALF + (rest % 4) * QUADS + rest // 4, i] = 1
    return expand.reshape(128, 512), perm


def swap_cores(x):
    return lax.ppermute(x, "core", [(0, 1), (1, 0)])


def along_y(x, d):
    return lax.ppermute(x, "y", [(a, (a + d) % 4) for a in range(4)])


def turn_grid(x, cross):
    def index(a, b, c, d, k):
        return (((a * 2 + b) * 4 + c) * 2 + d) * 2 + k

    moves = [
        (index(a, b, c, d, k), index(c, d, a, b, k ^ cross))
        for a in range(4)
        for b in range(2)
        for c in range(4)
        for d in range(2)
        for k in range(2)
    ]
    return lax.ppermute(x, ROW + COL, moves)


def to_all(x, axes, n):
    return lax.all_to_all(jnp.broadcast_to(x[None], (n,) + x.shape), axes, 0, 0, tiled=True)


def on_device(
    alignment_embedding,
    couplings_embedding,
    alignment_availability,
    amino_availability,
    alignment_scaling_vector,
    attention_joint_matrix,
    attention_final_matrix,
    coupling_scaling_vector,
    coupling_logit_matrix,
    tensor_scaling_vector,
    first_factor_matrix,
    second_factor_matrix,
    tensor_projection_matrix,
    tensor_offset_vector,
):
    core = lax.axis_index("core")
    at = jnp.stack([lax.axis_index(name) for name in ("y", "core")]).astype(jnp.int32)
    expand, perm = tables()

    bias = pair_bias(
        couplings_embedding.reshape(ROWS * COLS, PAIR),
        coupling_scaling_vector[None],
        coupling_logit_matrix.T,
    ).reshape(4 * HEADS, QUADS, 4 * COLS)
    bias = lax.all_to_all(bias, ROW + ("zh", "core"), 0, 0, tiled=True).reshape(8, 4, QUADS, 4 * COLS)

    keep = amino_availability.astype(F32)
    keep_i = lax.dynamic_slice_in_dim(keep, lax.axis_index(ROW) * ROWS, ROWS)
    keep_j = lax.dynamic_slice_in_dim(keep, lax.axis_index(COL) * COLS, COLS)
    keep_j = jnp.pad(keep_j, (0, 128 - COLS))[None]
    present = alignment_availability.astype(BF16)
    sent_mask = jnp.pad(
        jnp.stack([present[:, :128], jnp.pad(present[:, 128:], ((0, 0), (0, 64)))]), ((0, 0), (0, 4), (0, 0))
    ).reshape(16, 128)
    own, gate, keep_j = project(
        alignment_embedding,
        alignment_scaling_vector[None],
        attention_joint_matrix,
        jnp.asarray(expand, BF16),
        jnp.asarray(perm, BF16),
        sent_mask,
        keep_j,
    )
    own, bias, at, keep_i = lax.optimization_barrier((own, bias, at, keep_i))
    up, down = along_y(bias, 1), along_y(bias, 3)
    own = lax.all_to_all(own, ROW, 0, 0, tiled=True)
    own = lax.optimization_barrier((own, up, down))[0]
    pieces = (bias, up, down, along_y(up[:, :2], 1), along_y(down[:, 2:], 3))
    k, v, q = prepare(at, own, swap_cores(own))
    attended = attend(at, k, v, q, pieces).reshape(16, HALF, 128)
    attended = lax.all_to_all(attended, ROW + ("core",), 0, 0, tiled=True).reshape(HEADS, ROWS, 128)

    present = alignment_availability.astype(F32)
    alignment_refreshed, left, near, far = finish(
        at,
        attended,
        gate,
        alignment_embedding,
        attention_final_matrix,
        jnp.asarray(perm.T, BF16),
        tensor_scaling_vector[None],
        jnp.tile(first_factor_matrix, (1, 4)),
        jnp.tile(second_factor_matrix, (1, 4)),
        jnp.repeat(present.T, HEAD, axis=1),
    )
    left = lax.all_to_all(left, ("y", "zh"), 0, 0, tiled=True)
    right = jnp.stack([turn_grid(near, 0), turn_grid(far, 1)])
    right = to_all(right, ROW, 8)

    projection = (tensor_projection_matrix.astype(F32) / 64).astype(BF16)
    projection = projection.reshape(HEAD, 8, 4, PAIR).transpose(1, 2, 0, 3).reshape(1024, PAIR)
    couplings_refreshed = outer_update(
        at,
        left,
        swap_cores(left),
        right,
        projection,
        tensor_offset_vector[None],
        keep_i,
        keep_j,
        couplings_embedding,
    )
    return alignment_refreshed, couplings_refreshed


def solution(mesh):
    mesh = Mesh(mesh.devices.reshape(4, 2, 4, 2, 2), ROW + COL)
    placed = (P(COL, ROW, None), P(ROW, COL, None), P(COL, ROW)) + (P(),) * 11
    return jax.shard_map(
        on_device,
        mesh=mesh,
        in_specs=placed,
        out_specs=(P(COL, ROW, None), P(ROW, COL, None)),
        check_vma=False,
    )
```

```python
import jax
import jax.numpy as jnp
import numpy as np
from jax import lax
from jax.experimental import pallas as pl
from jax.experimental.pallas import tpu as pltpu
from jax.sharding import Mesh, PartitionSpec as P

F32 = jnp.float32
BF16 = jnp.bfloat16
HEADS = 8
HEAD = 32
SEQS = 4
ROWS = 192
HALF = 96
QUADS = 24
COLS = 96
EMB = 256
PAIR = 128
PEERS_COL = 16
TOTAL = 1536
CHUNK = 2
BIAS_AT = 48
EARLY = 1152
Q_ROWS, K_ROWS, V_ROWS, M_ROWS = 0, 192, 384, 576
SENT_ROWS = 592
LOG2E = 1.4426950408889634
ROW = ("x", "zl")
COL = ("y", "zh", "core")


def mm(a, b):
    return jnp.dot(a, b, preferred_element_type=F32)


def mm_tn(a, b):
    return lax.dot_general(a, b, (((0,), (0,)), ((), ())), preferred_element_type=F32)


def normalised(x, gain):
    mean = jnp.mean(x, axis=-1, keepdims=True)
    d = x - mean
    var = jnp.mean(d * d, axis=-1, keepdims=True)
    return (d * lax.rsqrt(var + 1e-05) * gain).astype(BF16)


def slot_of(shape):
    return (lax.broadcasted_iota(jnp.int32, shape, len(shape) - 1) // HEAD) % 4


def params(mib):
    return pltpu.CompilerParams(vmem_limit_bytes=mib * 1024 * 1024)


def vmem():
    return pl.BlockSpec(memory_space=pltpu.VMEM)


def smem():
    return pl.BlockSpec(memory_space=pltpu.SMEM)


def project_kernel(x_ref, g_ref, w_ref, e_ref, p_ref, m_ref, keep_ref, qkv_ref, gate_ref, column_ref):
    slot = slot_of((ROWS, 4 * 128))
    plain = [normalised(x_ref[s].astype(F32), g_ref[...]) for s in range(SEQS)]
    moved = [mm(p_ref[...], n).astype(BF16) for n in plain]
    for part in range(4):
        rows = moved if part in (0, 3) else plain
        for m in range(2):
            w = mm(w_ref[:, part * EMB + m * 128 : part * EMB + (m + 1) * 128], e_ref[...]).astype(BF16)
            acc = mm(rows[0], w)
            for s in range(1, SEQS):
                acc = jnp.where(slot == s, mm(rows[s], w), acc)
            for u in range(4):
                t = acc[:, u * 128 : (u + 1) * 128]
                h = 4 * m + u
                if part == 0:
                    qkv_ref[h, Q_ROWS:K_ROWS] = (t * HEAD ** (-0.5)).astype(BF16)
                elif part == 1:
                    qkv_ref[h, K_ROWS:V_ROWS] = t.astype(BF16)
                elif part == 2:
                    qkv_ref[h, V_ROWS:M_ROWS] = t.astype(BF16)
                else:
                    gate_ref[h] = jax.nn.sigmoid(t)
    for h in range(HEADS):
        qkv_ref[h, M_ROWS:] = m_ref[...]
    column_ref[...] = jnp.transpose(jnp.broadcast_to(keep_ref[...], (128, 128)))[:COLS]


def project(x, gain, w, expand, perm, present, keep):
    return pl.pallas_call(
        project_kernel,
        out_shape=(
            jax.ShapeDtypeStruct((HEADS, SENT_ROWS, 128), BF16),
            jax.ShapeDtypeStruct((HEADS, ROWS, 128), F32),
            jax.ShapeDtypeStruct((COLS, 128), F32),
        ),
        compiler_params=params(24),
        name="project",
    )(x, gain, w, expand, perm, present, keep)


def bias_kernel(z_ref, g_ref, w_ref, o_ref):
    acc = jnp.zeros((4 * COLS, 128), F32)
    head = lax.broadcasted_iota(jnp.int32, (HEADS, 128), 0)
    lane = lax.broadcasted_iota(jnp.int32, (HEADS, 128), 1)
    w = mm_tn(w_ref[...], jnp.where(lane // 16 == head, 1.0, 0.0).astype(BF16))
    group = lax.broadcasted_iota(jnp.int32, (PAIR, 128), 1) % 16
    for k in range(8):
        n = normalised(z_ref[768 * k : 768 * (k + 1)].astype(F32), g_ref[...])
        both = jnp.concatenate([n[:384], n[384:]], axis=1)
        spread = [jnp.where(group == 2 * k + e, w, 0.0).astype(BF16) for e in range(2)]
        acc += mm(both, jnp.concatenate(spread, axis=0))
    out = jnp.transpose(acc).astype(BF16).reshape(HEADS, 16, 4 * COLS)
    for copy in range(2):
        o_ref[:, copy] = out


def pair_bias(z, gain, w):
    return pl.pallas_call(
        bias_kernel,
        out_shape=jax.ShapeDtypeStruct((HEADS, 2, 2 * QUADS, 4 * COLS), BF16),
        grid=(3,),
        in_specs=[
            pl.BlockSpec((6144, PAIR), lambda t: (t, 0)),
            pl.BlockSpec((1, PAIR), lambda t: (0, 0)),
            pl.BlockSpec((HEADS, PAIR), lambda t: (0, 0)),
        ],
        out_specs=pl.BlockSpec((HEADS, 2, 16, 4 * COLS), lambda t: (0, 0, t, 0)),
        compiler_params=params(60),
        name="pair_bias",
    )(z, gain, w)


OFFSETS = (0, 3, 1, 2)


def prepare_kernel(at_ref, own_ref, par_ref, k_ref, v_ref, q_ref):
    y = at_ref[0]
    core = at_ref[1]
    for side, ref in enumerate((own_ref, par_ref)):
        for d in range(4):
            first = 2 * lax.rem(y + OFFSETS[d], 4)
            span = slice(384 * d, 384 * (d + 1))
            keys = jnp.concatenate([ref[first + e, K_ROWS:V_ROWS] for e in range(2)], axis=0)
            k_ref[side, :128, span] = jnp.transpose(keys.astype(F32)).astype(BF16)
            for e in range(2):
                v_ref[side, 384 * d + ROWS * e : 384 * d + ROWS * (e + 1), :128] = ref[first + e, V_ROWS:M_ROWS]
            masks = [ref[first + e, M_ROWS:].astype(F32) for e in range(2)]
            line = jnp.concatenate([masks[0][:8], masks[0][8:, :64], masks[1][:8], masks[1][8:, :64]], axis=1)
            absent = (line - 1.0) * 1000000000.0
            rows = []
            for s in range(SEQS):
                rows += [absent[s : s + 1], jnp.zeros((15, 384), F32)]
            k_ref[side, 128:192, span] = jnp.concatenate(rows, axis=0).astype(BF16)
        v_ref[side, :, 128:] = jnp.ones((TOTAL, 128), BF16)
        for r in range(8):
            q_ref[side, r] = ref[r, pl.ds(pl.multiple_of(core * HALF, HALF), HALF)]


def prepare(at, own, par):
    return pl.pallas_call(
        prepare_kernel,
        out_shape=(
            jax.ShapeDtypeStruct((2, 192, TOTAL), BF16),
            jax.ShapeDtypeStruct((2, TOTAL, EMB), BF16),
            jax.ShapeDtypeStruct((2, 8, HALF, 128), BF16),
        ),
        in_specs=[smem(), vmem(), vmem()],
        out_specs=(vmem(), vmem(), vmem()),
        compiler_params=params(24),
        name="prepare",
    )(at, own, par)


def attend_setup(pieces, rhs_pair, width):
    count = CHUNK * HALF
    for d, refs in enumerate(pieces):
        for r in range(CHUNK):
            got = [ref[r, k].astype(F32) for ref in refs for k in range(4 // len(refs))]
            lines = [
                jnp.concatenate([g[:, COLS * u : COLS * (u + 1)] for g in got], axis=1) for u in range(4)
            ]
            block = jnp.concatenate(lines, axis=0).astype(BF16)
            for rhs in rhs_pair:
                rhs[BIAS_AT + HALF * r : BIAS_AT + HALF * (r + 1), 384 * d : 384 * (d + 1)] = block
    for rhs in rhs_pair:
        rhs[BIAS_AT + count :] = jnp.zeros((EMB - BIAS_AT - count, width), BF16)


def attend_scores(k_ref, q_ref, width):
    count = CHUNK * HALF
    lane = lax.broadcasted_iota(jnp.int32, (count, 256), 1)
    row = lax.broadcasted_iota(jnp.int32, (count, 256), 0)
    pick = jnp.where((lane == HEAD) | (lane == row + BIAS_AT), 1.0, 0.0)
    first = lane[:, :128] < HEAD
    tail = pick[:, 128:].astype(BF16)

    def scores(out, rhs, side, s):
        rhs[:HEAD] = k_ref[side, HEAD * s : HEAD * (s + 1)]
        rhs[HEAD:BIAS_AT] = k_ref[side, 128 + 16 * s : 128 + 16 * (s + 1)]
        q = jnp.concatenate([q_ref[side, r] for r in range(CHUNK)], axis=0).astype(F32)
        if s:
            q = pltpu.roll(q, 128 - HEAD * s, 1)
        lhs = jnp.concatenate([jnp.where(first, q, pick[:, :128]).astype(BF16), tail], axis=1)
        top = None
        for at in range(0, width, 256):
            span = slice(at, min(at + 256, width))
            c = mm(lhs, rhs[:, span])
            out[:, span] = c
            for half in range(0, c.shape[1], 128):
                part = c[:, half : half + 128]
                top = part if top is None else jnp.maximum(top, part)
        return jnp.max(top, axis=1, keepdims=True)

    return scores


def attend_first_kernel(k_ref, v_ref, q_ref, b0, bp, bm, sum_ref, top_ref, rhs_even, rhs_odd, even, odd):
    count = CHUNK * HALF
    attend_setup(((b0,), (bp,), (bm,)), (rhs_even, rhs_odd), EARLY)
    scores = attend_scores(k_ref, q_ref, EARLY)
    wide = slot_of((count, 256))
    top = scores(even, rhs_even, 0, 0)
    for n in range(2 * SEQS):
        side, s = divmod(n, SEQS)
        now, later, rhs = (even, odd, rhs_odd) if n % 2 == 0 else (odd, even, rhs_even)
        if n < 2 * SEQS - 1:
            following = scores(later, rhs, *divmod(n + 1, SEQS))
        got = mm(jnp.exp(now[...] - top).astype(BF16), v_ref[side])
        total = got if s == 0 else jnp.where(wide == s, got, total)
        top_ref[side, s] = jnp.broadcast_to(top, (count, 128))
        if n < 2 * SEQS - 1:
            top = following
        if s == SEQS - 1:
            sum_ref[side] = total


def attend_last_kernel(at_ref, k_ref, v_ref, q_ref, f1, f2, sum_ref, top_ref, o_ref, rhs_all, buf_all):
    core = at_ref[1]
    count = CHUNK * HALF
    late = TOTAL - EARLY
    attend_setup(((f1, f2),), [rhs_all.at[n] for n in range(2 * SEQS)], late)
    scores = attend_scores(k_ref, q_ref, late)
    wide = slot_of((count, 256))
    peaks = [scores(buf_all.at[n], rhs_all.at[n], *divmod(n, SEQS)) for n in range(2 * SEQS)]
    for n in range(2 * SEQS):
        side, s = divmod(n, SEQS)
        before = top_ref[side, s]
        peak = jnp.maximum(peaks[n], before)
        e = jnp.exp(buf_all[n] - jnp.concatenate([peak] * (late // 128), axis=1)).astype(BF16)
        shrink = jnp.exp(before - peak)
        got = mm(e, v_ref[side]) + sum_ref[side] * jnp.concatenate([shrink, shrink], axis=1)
        total = got if s == 0 else jnp.where(wide == s, got, total)
        if s == SEQS - 1:
            out = (total[:, :128] / total[:, 128:]).astype(BF16)
            quad = core if side == 0 else 1 - core
            for r in range(CHUNK):
                o_ref[r, quad] = out[HALF * r : HALF * (r + 1)]


def attend(at, k, v, q, pieces):
    count = CHUNK * HALF
    late = TOTAL - EARLY

    def piece(parts):
        return pl.BlockSpec((CHUNK, parts, QUADS, 4 * COLS), lambda t: (t, 0, 0, 0))

    def scratch(width):
        return [pltpu.VMEM((EMB, width), BF16)] * 2 + [pltpu.VMEM((count, width), F32)] * 2

    queries = pl.BlockSpec((2, CHUNK, HALF, 128), lambda t: (0, t, 0, 0))
    sums = pl.BlockSpec((2, count, 256), lambda t: (0, t, 0))
    tops = pl.BlockSpec((2, SEQS, count, 128), lambda t: (0, 0, t, 0))
    total, top = pl.pallas_call(
        attend_first_kernel,
        out_shape=(
            jax.ShapeDtypeStruct((2, 8 * HALF, 256), F32),
            jax.ShapeDtypeStruct((2, SEQS, 8 * HALF, 128), F32),
        ),
        grid=(8 // CHUNK,),
        in_specs=[
            pl.BlockSpec((2, 192, EARLY), lambda t: (0, 0, 0)),
            pl.BlockSpec((2, EARLY, EMB), lambda t: (0, 0, 0)),
            queries,
            piece(4),
            piece(4),
            piece(4),
        ],
        out_specs=(sums, tops),
        scratch_shapes=scratch(EARLY),
        compiler_params=params(28),
        name="attend_first",
    )(k, v, q, *pieces[:3])
    return pl.pallas_call(
        attend_last_kernel,
        out_shape=jax.ShapeDtypeStruct((8, 2, HALF, 128), BF16),
        grid=(8 // CHUNK,),
        in_specs=[
            smem(),
            pl.BlockSpec((2, 192, late), lambda t: (0, 0, EARLY // late)),
            pl.BlockSpec((2, late, EMB), lambda t: (0, EARLY // late, 0)),
            queries,
            piece(2),
            piece(2),
            sums,
            tops,
        ],
        out_specs=pl.BlockSpec((CHUNK, 2, HALF, 128), lambda t: (t, 0, 0, 0)),
        scratch_shapes=[pltpu.VMEM((2 * SEQS, EMB, late), BF16), pltpu.VMEM((2 * SEQS, count, late), F32)],
        compiler_params=params(28),
        name="attend_last",
    )(at, k, v, q, *pieces[3:], total, top)


def finish_kernel(
    att_ref, gate_ref, x_ref, wf_ref, pinv_ref, g_ref, wl_ref, wr_ref, ac_ref, new_ref, left_ref, right_ref
):
    gated = jnp.concatenate(
        [(gate_ref[h] * att_ref[h].astype(F32)).astype(BF16) for h in range(HEADS)], axis=1
    )
    gated = mm(pinv_ref[...], gated)
    w = jnp.concatenate([wf_ref[HEAD * (k // 4) : HEAD * (k // 4 + 1)] for k in range(4 * HEADS)], axis=0)
    slot = slot_of((ROWS, 4 * EMB))
    slot_one = slot_of((ROWS, 128))
    left = jnp.zeros((ROWS, 128), F32)
    right = jnp.zeros((ROWS, 128), F32)
    for s in range(SEQS):
        inc = mm(jnp.where(slot == s, gated, 0.0).astype(BF16), w)
        new = (x_ref[s].astype(F32) + inc).astype(BF16)
        new_ref[s] = new
        n = normalised(new.astype(F32), g_ref[...])
        left = jnp.where(slot_one == s, mm(n, wl_ref[...]), left)
        right = jnp.where(slot_one == s, mm(n, wr_ref[...]), right)
    right_ref[...] = (right * ac_ref[...]).astype(BF16)
    left = (left * ac_ref[...]).astype(BF16)
    for copy in range(PEERS_COL // 2):
        left_ref[copy] = left


def finish(*args):
    return pl.pallas_call(
        finish_kernel,
        out_shape=(
            jax.ShapeDtypeStruct((SEQS, ROWS, EMB), BF16),
            jax.ShapeDtypeStruct((PEERS_COL // 2, ROWS, 128), BF16),
            jax.ShapeDtypeStruct((ROWS, 128), BF16),
        ),
        compiler_params=params(24),
        name="finish",
    )(*args)


STEP = 64
PART = 16


def outer_kernel(at_ref, lo_ref, lp_ref, r_ref, w_ref, off_ref, ki_ref, kj_ref, z_ref, o_ref, l_all, r_all, lhs, rhs, *obf):
    step = pl.program_id(0)

    @pl.when(step == 0)
    def _():
        core = at_ref[1]
        pad = jnp.zeros((128 - COLS, 128), F32)
        for p in range(PEERS_COL // 2):
            for side, ref in enumerate((lo_ref, lp_ref)):
                c = 2 * p + (core if side == 0 else 1 - core)
                l_all[pl.ds(pl.multiple_of(c * ROWS, ROWS), ROWS)] = ref[p].astype(F32)
        for c in range(PEERS_COL):
            r_all[128 * c : 128 * (c + 1)] = jnp.transpose(jnp.concatenate([r_ref[c].astype(F32), pad], axis=0))
        for q in range(8):
            lines = [
                r_all[pl.ds(HEAD * s + 4 * q + b, PEERS_COL, stride=128), :] for b in range(4) for s in range(SEQS)
            ]
            turned = jnp.transpose(jnp.concatenate(lines, axis=0))
            lhs[COLS * q : COLS * (q + 1)] = turned[:COLS].astype(BF16)

    slot = slot_of((PEERS_COL, 128))
    for k in range(STEP):
        m = l_all[pl.ds(step * STEP + k, PEERS_COL, stride=ROWS), :]
        rolled = [m] + [pltpu.roll(m, HEAD * d, 1) for d in range(1, 4)]
        for b in range(4):
            for s in range(SEQS):
                at = 64 * b + 16 * s
                rhs[at : at + 16, 128 * k : 128 * (k + 1)] = jnp.where(slot == b, rolled[(b - s) % 4], 0.0).astype(BF16)

    def products(part):
        for k in range(0, PART, 2):
            at = 128 * (PART * part + k)
            outer = mm(lhs[...], rhs[:, at : at + 256]).astype(BF16)
            for e in range(2):
                for q in range(8):
                    obf[part % 2][COLS * (k + e) : COLS * (k + e + 1), 128 * q : 128 * (q + 1)] = outer[
                        COLS * q : COLS * (q + 1), 128 * e : 128 * (e + 1)
                    ]

    def project_part(part):
        update = mm(obf[part % 2][...], w_ref[...]) + off_ref[...]
        for k in range(PART):
            i = PART * part + k
            keep = kj_ref[...] * ki_ref[step * STEP + i]
            o_ref[i] = (z_ref[i].astype(F32) + update[COLS * k : COLS * (k + 1)] * keep).astype(BF16)

    products(0)
    for part in range(1, STEP // PART):
        products(part)
        project_part(part - 1)
    project_part(STEP // PART - 1)


def outer_update(at, left_own, left_par, right, w, offset, keep_i, keep_j, z):
    return pl.pallas_call(
        outer_kernel,
        out_shape=jax.ShapeDtypeStruct((ROWS, COLS, PAIR), BF16),
        grid=(ROWS // STEP,),
        in_specs=[
            smem(),
            pl.BlockSpec((PEERS_COL // 2, ROWS, 128), lambda t: (0, 0, 0)),
            pl.BlockSpec((PEERS_COL // 2, ROWS, 128), lambda t: (0, 0, 0)),
            pl.BlockSpec((PEERS_COL, COLS, 128), lambda t: (0, 0, 0)),
            pl.BlockSpec((1024, PAIR), lambda t: (0, 0)),
            pl.BlockSpec((1, PAIR), lambda t: (0, 0)),
            smem(),
            pl.BlockSpec((COLS, PAIR), lambda t: (0, 0)),
            pl.BlockSpec((STEP, COLS, PAIR), lambda t: (t, 0, 0)),
        ],
        out_specs=pl.BlockSpec((STEP, COLS, PAIR), lambda t: (t, 0, 0)),
        scratch_shapes=[
            pltpu.VMEM((PEERS_COL * ROWS, 128), F32),
            pltpu.VMEM((PEERS_COL * 128, 128), F32),
            pltpu.VMEM((8 * COLS, EMB), BF16),
            pltpu.VMEM((256, 128 * STEP), BF16),
            pltpu.VMEM((PART * COLS, 1024), BF16),
            pltpu.VMEM((PART * COLS, 1024), BF16),
        ],
        compiler_params=params(63),
        name="outer_update",
    )(at, left_own, left_par, right, w, offset, keep_i, keep_j, z)


def tables():
    expand = np.zeros((128, 4, 4, HEAD), np.float32)
    for u in range(4):
        for d in range(HEAD):
            expand[u * HEAD + d, u, :, d] = 1
    perm = np.zeros((ROWS, ROWS), np.float32)
    for i in range(ROWS):
        half, rest = divmod(i, HALF)
        perm[half * HALF + (rest % 4) * QUADS + rest // 4, i] = 1
    return expand.reshape(128, 512), perm


def swap_cores(x):
    return lax.ppermute(x, "core", [(0, 1), (1, 0)])


def along_y(x, d):
    return lax.ppermute(x, "y", [(a, (a + d) % 4) for a in range(4)])


def turn_grid(x):
    def index(a, b, c, d):
        return ((a * 2 + b) * 4 + c) * 2 + d

    moves = [
        (index(a, b, c, d), index(c, d, a, b)) for a in range(4) for b in range(2) for c in range(4) for d in range(2)
    ]
    return lax.ppermute(x, ("x", "zl", "y", "zh"), moves)


def on_device(
    alignment_embedding,
    couplings_embedding,
    alignment_availability,
    amino_availability,
    alignment_scaling_vector,
    attention_joint_matrix,
    attention_final_matrix,
    coupling_scaling_vector,
    coupling_logit_matrix,
    tensor_scaling_vector,
    first_factor_matrix,
    second_factor_matrix,
    tensor_projection_matrix,
    tensor_offset_vector,
):
    core = lax.axis_index("core")
    at = jnp.stack([lax.axis_index(name) for name in ("y", "core")]).astype(jnp.int32)
    expand, perm = tables()

    bias = pair_bias(
        couplings_embedding.reshape(ROWS * COLS, PAIR),
        coupling_scaling_vector[None],
        coupling_logit_matrix.T,
    ).reshape(4 * HEADS, QUADS, 4 * COLS)
    bias = lax.all_to_all(bias, ROW + ("zh", "core"), 0, 0, tiled=True).reshape(8, 4, QUADS, 4 * COLS)

    keep = amino_availability.astype(F32)
    keep_i = lax.dynamic_slice_in_dim(keep, lax.axis_index(ROW) * ROWS, ROWS)
    keep_j = lax.dynamic_slice_in_dim(keep, lax.axis_index(COL) * COLS, COLS)
    keep_j = jnp.pad(keep_j, (0, 128 - COLS))[None]
    present = alignment_availability.astype(BF16)
    sent_mask = jnp.pad(
        jnp.stack([present[:, :128], jnp.pad(present[:, 128:], ((0, 0), (0, 64)))]), ((0, 0), (0, 4), (0, 0))
    ).reshape(16, 128)
    own, gate, keep_j = project(
        alignment_embedding,
        alignment_scaling_vector[None],
        attention_joint_matrix,
        jnp.asarray(expand, BF16),
        jnp.asarray(perm, BF16),
        sent_mask,
        keep_j,
    )
    own, bias, at, keep_i = lax.optimization_barrier((own, bias, at, keep_i))
    up, down = along_y(bias, 1), along_y(bias, 3)
    own = lax.all_to_all(own, ROW, 0, 0, tiled=True)
    own = lax.optimization_barrier((own, up, down))[0]
    pieces = (bias, up, down, along_y(up[:, :2], 1), along_y(down[:, 2:], 3))
    k, v, q = prepare(at, own, swap_cores(own))
    attended = attend(at, k, v, q, pieces).reshape(16, HALF, 128)
    attended = lax.all_to_all(attended, ROW + ("core",), 0, 0, tiled=True).reshape(HEADS, ROWS, 128)

    present = alignment_availability.astype(F32)
    alignment_refreshed, left, right = finish(
        attended,
        gate,
        alignment_embedding,
        attention_final_matrix,
        jnp.asarray(perm.T, BF16),
        tensor_scaling_vector[None],
        jnp.tile(first_factor_matrix, (1, 4)),
        jnp.tile(second_factor_matrix, (1, 4)),
        jnp.repeat(present.T, HEAD, axis=1),
    )
    left = lax.all_to_all(left, ("y", "zh"), 0, 0, tiled=True)
    right = jnp.broadcast_to(turn_grid(right)[None], (8, ROWS, 128)).reshape(PEERS_COL, COLS, 128)
    right = lax.all_to_all(right, ROW + ("core",), 0, 0, tiled=True)

    projection = (tensor_projection_matrix.astype(F32) / 64).astype(BF16)
    projection = projection.reshape(HEAD, 8, 4, PAIR).transpose(1, 2, 0, 3).reshape(1024, PAIR)
    couplings_refreshed = outer_update(
        at,
        left,
        swap_cores(left),
        right,
        projection,
        tensor_offset_vector[None],
        keep_i,
        keep_j,
        couplings_embedding,
    )
    return alignment_refreshed, couplings_refreshed


def solution(mesh):
    mesh = Mesh(mesh.devices.reshape(4, 2, 4, 2, 2), ROW + COL)
    placed = (P(COL, ROW, None), P(ROW, COL, None), P(COL, ROW)) + (P(),) * 11
    return jax.shard_map(
        on_device,
        mesh=mesh,
        in_specs=placed,
        out_specs=(P(COL, ROW, None), P(ROW, COL, None)),
        check_vma=False,
    )
```

```python
import jax
import jax.numpy as jnp
import numpy as np
from jax import lax
from jax.experimental import pallas as pl
from jax.experimental.pallas import tpu as pltpu
from jax.sharding import Mesh, PartitionSpec as P

F32 = jnp.float32
BF16 = jnp.bfloat16
HEADS = 8
HEAD = 32
SEQS = 4
ROWS = 192
HALF = 96
QUADS = 24
COLS = 96
EMB = 256
PAIR = 128
PEERS_COL = 16
TOTAL = 1536
CHUNK = 2
BIAS_AT = 48
EARLY = 1152
Q_ROWS, K_ROWS, V_ROWS, M_ROWS = 0, 192, 384, 576
SENT_ROWS = 592
LOG2E = 1.4426950408889634
ROW = ("x", "zl")
COL = ("y", "zh", "core")


def mm(a, b):
    return jnp.dot(a, b, preferred_element_type=F32)


def mm_tn(a, b):
    return lax.dot_general(a, b, (((0,), (0,)), ((), ())), preferred_element_type=F32)


def normalised(x, gain):
    mean = jnp.mean(x, axis=-1, keepdims=True)
    d = x - mean
    var = jnp.mean(d * d, axis=-1, keepdims=True)
    return (d * lax.rsqrt(var + 1e-05) * gain).astype(BF16)


def slot_of(shape):
    return (lax.broadcasted_iota(jnp.int32, shape, len(shape) - 1) // HEAD) % 4


def params(mib):
    return pltpu.CompilerParams(vmem_limit_bytes=mib * 1024 * 1024)


def vmem():
    return pl.BlockSpec(memory_space=pltpu.VMEM)


def smem():
    return pl.BlockSpec(memory_space=pltpu.SMEM)


def project_kernel(x_ref, g_ref, w_ref, e_ref, p_ref, m_ref, keep_ref, qkv_ref, gate_ref, column_ref):
    slot = slot_of((ROWS, 4 * 128))
    plain = [normalised(x_ref[s].astype(F32), g_ref[...]) for s in range(SEQS)]
    moved = [mm(p_ref[...], n).astype(BF16) for n in plain]
    for part in range(4):
        rows = moved if part in (0, 3) else plain
        for m in range(2):
            w = mm(w_ref[:, part * EMB + m * 128 : part * EMB + (m + 1) * 128], e_ref[...]).astype(BF16)
            acc = mm(rows[0], w)
            for s in range(1, SEQS):
                acc = jnp.where(slot == s, mm(rows[s], w), acc)
            for u in range(4):
                t = acc[:, u * 128 : (u + 1) * 128]
                h = 4 * m + u
                if part == 0:
                    qkv_ref[h, Q_ROWS:K_ROWS] = (t * HEAD ** (-0.5)).astype(BF16)
                elif part == 1:
                    qkv_ref[h, K_ROWS:V_ROWS] = t.astype(BF16)
                elif part == 2:
                    qkv_ref[h, V_ROWS:M_ROWS] = t.astype(BF16)
                else:
                    gate_ref[h] = jax.nn.sigmoid(t)
    for h in range(HEADS):
        qkv_ref[h, M_ROWS:] = m_ref[...]
    column_ref[...] = jnp.transpose(jnp.broadcast_to(keep_ref[...], (128, 128)))[:COLS]


def project(x, gain, w, expand, perm, present, keep):
    return pl.pallas_call(
        project_kernel,
        out_shape=(
            jax.ShapeDtypeStruct((HEADS, SENT_ROWS, 128), BF16),
            jax.ShapeDtypeStruct((HEADS, ROWS, 128), F32),
            jax.ShapeDtypeStruct((COLS, 128), F32),
        ),
        compiler_params=params(24),
        name="project",
    )(x, gain, w, expand, perm, present, keep)


def bias_kernel(z_ref, g_ref, w_ref, o_ref):
    acc = jnp.zeros((4 * COLS, 128), F32)
    head = lax.broadcasted_iota(jnp.int32, (HEADS, 128), 0)
    lane = lax.broadcasted_iota(jnp.int32, (HEADS, 128), 1)
    w = mm_tn(w_ref[...], jnp.where(lane // 16 == head, 1.0, 0.0).astype(BF16))
    group = lax.broadcasted_iota(jnp.int32, (PAIR, 128), 1) % 16
    for k in range(8):
        n = normalised(z_ref[768 * k : 768 * (k + 1)].astype(F32), g_ref[...])
        both = jnp.concatenate([n[:384], n[384:]], axis=1)
        spread = [jnp.where(group == 2 * k + e, w, 0.0).astype(BF16) for e in range(2)]
        acc += mm(both, jnp.concatenate(spread, axis=0))
    out = jnp.transpose(acc).astype(BF16).reshape(HEADS, 16, 4 * COLS)
    for copy in range(2):
        o_ref[:, copy] = out


def pair_bias(z, gain, w):
    return pl.pallas_call(
        bias_kernel,
        out_shape=jax.ShapeDtypeStruct((HEADS, 2, 2 * QUADS, 4 * COLS), BF16),
        grid=(3,),
        in_specs=[
            pl.BlockSpec((6144, PAIR), lambda t: (t, 0)),
            pl.BlockSpec((1, PAIR), lambda t: (0, 0)),
            pl.BlockSpec((HEADS, PAIR), lambda t: (0, 0)),
        ],
        out_specs=pl.BlockSpec((HEADS, 2, 16, 4 * COLS), lambda t: (0, 0, t, 0)),
        compiler_params=params(60),
        name="pair_bias",
    )(z, gain, w)


OFFSETS = (0, 3, 1, 2)


def prepare_kernel(at_ref, own_ref, par_ref, k_ref, v_ref, q_ref):
    y = at_ref[0]
    core = at_ref[1]
    for side, ref in enumerate((own_ref, par_ref)):
        for d in range(4):
            first = 2 * lax.rem(y + OFFSETS[d], 4)
            span = slice(384 * d, 384 * (d + 1))
            keys = jnp.concatenate([ref[first + e, K_ROWS:V_ROWS] for e in range(2)], axis=0)
            k_ref[side, :128, span] = jnp.transpose(keys.astype(F32)).astype(BF16)
            for e in range(2):
                v_ref[side, 384 * d + ROWS * e : 384 * d + ROWS * (e + 1), :128] = ref[first + e, V_ROWS:M_ROWS]
            masks = [ref[first + e, M_ROWS:].astype(F32) for e in range(2)]
            line = jnp.concatenate([masks[0][:8], masks[0][8:, :64], masks[1][:8], masks[1][8:, :64]], axis=1)
            absent = (line - 1.0) * 1000000000.0
            rows = []
            for s in range(SEQS):
                rows += [absent[s : s + 1], jnp.zeros((15, 384), F32)]
            k_ref[side, 128:192, span] = jnp.concatenate(rows, axis=0).astype(BF16)
        v_ref[side, :, 128:] = jnp.ones((TOTAL, 128), BF16)
        for r in range(8):
            q_ref[side, r] = ref[r, pl.ds(pl.multiple_of(core * HALF, HALF), HALF)]


def prepare(at, own, par):
    return pl.pallas_call(
        prepare_kernel,
        out_shape=(
            jax.ShapeDtypeStruct((2, 192, TOTAL), BF16),
            jax.ShapeDtypeStruct((2, TOTAL, EMB), BF16),
            jax.ShapeDtypeStruct((2, 8, HALF, 128), BF16),
        ),
        in_specs=[smem(), vmem(), vmem()],
        out_specs=(vmem(), vmem(), vmem()),
        compiler_params=params(24),
        name="prepare",
    )(at, own, par)


def attend_setup(pieces, rhs_pair, width):
    count = CHUNK * HALF
    for d, refs in enumerate(pieces):
        for r in range(CHUNK):
            got = [ref[r, k].astype(F32) for ref in refs for k in range(4 // len(refs))]
            lines = [
                jnp.concatenate([g[:, COLS * u : COLS * (u + 1)] for g in got], axis=1) for u in range(4)
            ]
            block = jnp.concatenate(lines, axis=0).astype(BF16)
            for rhs in rhs_pair:
                rhs[BIAS_AT + HALF * r : BIAS_AT + HALF * (r + 1), 384 * d : 384 * (d + 1)] = block
    for rhs in rhs_pair:
        rhs[BIAS_AT + count :] = jnp.zeros((EMB - BIAS_AT - count, width), BF16)


def attend_scores(k_ref, q_ref, width):
    count = CHUNK * HALF
    lane = lax.broadcasted_iota(jnp.int32, (count, 256), 1)
    row = lax.broadcasted_iota(jnp.int32, (count, 256), 0)
    pick = jnp.where((lane == HEAD) | (lane == row + BIAS_AT), 1.0, 0.0)
    first = lane[:, :128] < HEAD
    tail = pick[:, 128:].astype(BF16)

    def scores(out, rhs, side, s):
        rhs[:HEAD] = k_ref[side, HEAD * s : HEAD * (s + 1)]
        rhs[HEAD:BIAS_AT] = k_ref[side, 128 + 16 * s : 128 + 16 * (s + 1)]
        q = jnp.concatenate([q_ref[side, r] for r in range(CHUNK)], axis=0).astype(F32)
        if s:
            q = pltpu.roll(q, 128 - HEAD * s, 1)
        lhs = jnp.concatenate([jnp.where(first, q, pick[:, :128]).astype(BF16), tail], axis=1)
        top = None
        for at in range(0, width, 256):
            span = slice(at, min(at + 256, width))
            c = mm(lhs, rhs[:, span])
            out[:, span] = c
            for half in range(0, c.shape[1], 128):
                part = c[:, half : half + 128]
                top = part if top is None else jnp.maximum(top, part)
        return jnp.max(top, axis=1, keepdims=True)

    return scores


def attend_first_kernel(k_ref, v_ref, q_ref, b0, bp, bm, sum_ref, top_ref, rhs_even, rhs_odd, even, odd):
    count = CHUNK * HALF
    attend_setup(((b0,), (bp,), (bm,)), (rhs_even, rhs_odd), EARLY)
    scores = attend_scores(k_ref, q_ref, EARLY)
    wide = slot_of((count, 256))
    top = scores(even, rhs_even, 0, 0)
    for n in range(2 * SEQS):
        side, s = divmod(n, SEQS)
        now, later, rhs = (even, odd, rhs_odd) if n % 2 == 0 else (odd, even, rhs_even)
        if n < 2 * SEQS - 1:
            following = scores(later, rhs, *divmod(n + 1, SEQS))
        got = mm(jnp.exp(now[...] - top).astype(BF16), v_ref[side])
        total = got if s == 0 else jnp.where(wide == s, got, total)
        top_ref[side, s] = jnp.broadcast_to(top, (count, 128))
        if n < 2 * SEQS - 1:
            top = following
        if s == SEQS - 1:
            sum_ref[side] = total


def attend_last_kernel(at_ref, k_ref, v_ref, q_ref, f1, f2, sum_ref, top_ref, o_ref, rhs_all, buf_all):
    core = at_ref[1]
    count = CHUNK * HALF
    late = TOTAL - EARLY
    attend_setup(((f1, f2),), [rhs_all.at[n] for n in range(2 * SEQS)], late)
    scores = attend_scores(k_ref, q_ref, late)
    wide = slot_of((count, 256))
    peaks = [scores(buf_all.at[n], rhs_all.at[n], *divmod(n, SEQS)) for n in range(2 * SEQS)]
    for n in range(2 * SEQS):
        side, s = divmod(n, SEQS)
        before = top_ref[side, s]
        peak = jnp.maximum(peaks[n], before)
        e = jnp.exp(buf_all[n] - jnp.concatenate([peak] * (late // 128), axis=1)).astype(BF16)
        shrink = jnp.exp(before - peak)
        got = mm(e, v_ref[side]) + sum_ref[side] * jnp.concatenate([shrink, shrink], axis=1)
        total = got if s == 0 else jnp.where(wide == s, got, total)
        if s == SEQS - 1:
            out = (total[:, :128] / total[:, 128:]).astype(BF16)
            quad = core if side == 0 else 1 - core
            for r in range(CHUNK):
                o_ref[r, quad] = out[HALF * r : HALF * (r + 1)]


def attend(at, k, v, q, pieces):
    count = CHUNK * HALF
    late = TOTAL - EARLY

    def piece(parts):
        return pl.BlockSpec((CHUNK, parts, QUADS, 4 * COLS), lambda t: (t, 0, 0, 0))

    def scratch(width):
        return [pltpu.VMEM((EMB, width), BF16)] * 2 + [pltpu.VMEM((count, width), F32)] * 2

    queries = pl.BlockSpec((2, CHUNK, HALF, 128), lambda t: (0, t, 0, 0))
    sums = pl.BlockSpec((2, count, 256), lambda t: (0, t, 0))
    tops = pl.BlockSpec((2, SEQS, count, 128), lambda t: (0, 0, t, 0))
    total, top = pl.pallas_call(
        attend_first_kernel,
        out_shape=(
            jax.ShapeDtypeStruct((2, 8 * HALF, 256), F32),
            jax.ShapeDtypeStruct((2, SEQS, 8 * HALF, 128), F32),
        ),
        grid=(8 // CHUNK,),
        in_specs=[
            pl.BlockSpec((2, 192, EARLY), lambda t: (0, 0, 0)),
            pl.BlockSpec((2, EARLY, EMB), lambda t: (0, 0, 0)),
            queries,
            piece(4),
            piece(4),
            piece(4),
        ],
        out_specs=(sums, tops),
        scratch_shapes=scratch(EARLY),
        compiler_params=params(28),
        name="attend_first",
    )(k, v, q, *pieces[:3])
    return pl.pallas_call(
        attend_last_kernel,
        out_shape=jax.ShapeDtypeStruct((8, 2, HALF, 128), BF16),
        grid=(8 // CHUNK,),
        in_specs=[
            smem(),
            pl.BlockSpec((2, 192, late), lambda t: (0, 0, EARLY // late)),
            pl.BlockSpec((2, late, EMB), lambda t: (0, EARLY // late, 0)),
            queries,
            piece(2),
            piece(2),
            sums,
            tops,
        ],
        out_specs=pl.BlockSpec((CHUNK, 2, HALF, 128), lambda t: (t, 0, 0, 0)),
        scratch_shapes=[pltpu.VMEM((2 * SEQS, EMB, late), BF16), pltpu.VMEM((2 * SEQS, count, late), F32)],
        compiler_params=params(28),
        name="attend_last",
    )(at, k, v, q, *pieces[3:], total, top)


def finish_kernel(
    att_ref, gate_ref, x_ref, wf_ref, pinv_ref, g_ref, wl_ref, wr_ref, ac_ref, new_ref, left_ref, right_ref
):
    gated = jnp.concatenate(
        [(gate_ref[h] * att_ref[h].astype(F32)).astype(BF16) for h in range(HEADS)], axis=1
    )
    gated = mm(pinv_ref[...], gated)
    w = jnp.concatenate([wf_ref[HEAD * (k // 4) : HEAD * (k // 4 + 1)] for k in range(4 * HEADS)], axis=0)
    slot = slot_of((ROWS, 4 * EMB))
    slot_one = slot_of((ROWS, 128))
    left = jnp.zeros((ROWS, 128), F32)
    right = jnp.zeros((ROWS, 128), F32)
    for s in range(SEQS):
        inc = mm(jnp.where(slot == s, gated, 0.0).astype(BF16), w)
        new = (x_ref[s].astype(F32) + inc).astype(BF16)
        new_ref[s] = new
        n = normalised(new.astype(F32), g_ref[...])
        left = jnp.where(slot_one == s, mm(n, wl_ref[...]), left)
        right = jnp.where(slot_one == s, mm(n, wr_ref[...]), right)
    right_ref[...] = (right * ac_ref[...]).astype(BF16)
    left = (left * ac_ref[...]).astype(BF16)
    for copy in range(PEERS_COL // 2):
        left_ref[copy] = left


def finish(*args):
    return pl.pallas_call(
        finish_kernel,
        out_shape=(
            jax.ShapeDtypeStruct((SEQS, ROWS, EMB), BF16),
            jax.ShapeDtypeStruct((PEERS_COL // 2, ROWS, 128), BF16),
            jax.ShapeDtypeStruct((ROWS, 128), BF16),
        ),
        compiler_params=params(24),
        name="finish",
    )(*args)


STEP = 64
PART = 16


def lines_kernel(at_ref, lo_ref, lp_ref, o_ref):
    core = at_ref[1]
    for p in range(PEERS_COL // 2):
        for side, ref in enumerate((lo_ref, lp_ref)):
            c = 2 * p + (core if side == 0 else 1 - core)
            o_ref[pl.ds(pl.multiple_of(c * ROWS, ROWS), ROWS)] = ref[p].astype(F32)


def lines(at, left_own, left_par):
    return pl.pallas_call(
        lines_kernel,
        out_shape=jax.ShapeDtypeStruct((PEERS_COL * ROWS, 128), F32),
        in_specs=[smem(), vmem(), vmem()],
        out_specs=vmem(),
        compiler_params=params(16),
        name="lines",
    )(at, left_own, left_par)


def outer_kernel(l_all, r_ref, w_ref, off_ref, ki_ref, kj_ref, z_ref, o_ref, r_all, lhs, rhs, *obf):
    step = pl.program_id(0)

    @pl.when(step == 0)
    def _():
        pad = jnp.zeros((128 - COLS, 128), F32)
        for c in range(PEERS_COL):
            r_all[128 * c : 128 * (c + 1)] = jnp.transpose(jnp.concatenate([r_ref[c].astype(F32), pad], axis=0))
        for q in range(8):
            lines = [
                r_all[pl.ds(HEAD * s + 4 * q + b, PEERS_COL, stride=128), :] for b in range(4) for s in range(SEQS)
            ]
            turned = jnp.transpose(jnp.concatenate(lines, axis=0))
            lhs[COLS * q : COLS * (q + 1)] = turned[:COLS].astype(BF16)

    slot = slot_of((PEERS_COL, 128))
    for k in range(STEP):
        m = l_all[pl.ds(step * STEP + k, PEERS_COL, stride=ROWS), :]
        rolled = [m] + [pltpu.roll(m, HEAD * d, 1) for d in range(1, 4)]
        for b in range(4):
            for s in range(SEQS):
                at = 64 * b + 16 * s
                rhs[at : at + 16, 128 * k : 128 * (k + 1)] = jnp.where(slot == b, rolled[(b - s) % 4], 0.0).astype(BF16)

    def products(part):
        for k in range(0, PART, 2):
            at = 128 * (PART * part + k)
            outer = mm(lhs[...], rhs[:, at : at + 256]).astype(BF16)
            for e in range(2):
                for q in range(8):
                    obf[part % 2][COLS * (k + e) : COLS * (k + e + 1), 128 * q : 128 * (q + 1)] = outer[
                        COLS * q : COLS * (q + 1), 128 * e : 128 * (e + 1)
                    ]

    def project_part(part):
        update = mm(obf[part % 2][...], w_ref[...]) + off_ref[...]
        for k in range(PART):
            i = PART * part + k
            keep = kj_ref[...] * ki_ref[step * STEP + i]
            o_ref[i] = (z_ref[i].astype(F32) + update[COLS * k : COLS * (k + 1)] * keep).astype(BF16)

    products(0)
    for part in range(1, STEP // PART):
        products(part)
        project_part(part - 1)
    project_part(STEP // PART - 1)


def outer_update(left, right, w, offset, keep_i, keep_j, z):
    return pl.pallas_call(
        outer_kernel,
        out_shape=jax.ShapeDtypeStruct((ROWS, COLS, PAIR), BF16),
        grid=(ROWS // STEP,),
        in_specs=[
            pl.BlockSpec((PEERS_COL * ROWS, 128), lambda t: (0, 0)),
            pl.BlockSpec((PEERS_COL, COLS, 128), lambda t: (0, 0, 0)),
            pl.BlockSpec((1024, PAIR), lambda t: (0, 0)),
            pl.BlockSpec((1, PAIR), lambda t: (0, 0)),
            smem(),
            pl.BlockSpec((COLS, PAIR), lambda t: (0, 0)),
            pl.BlockSpec((STEP, COLS, PAIR), lambda t: (t, 0, 0)),
        ],
        out_specs=pl.BlockSpec((STEP, COLS, PAIR), lambda t: (t, 0, 0)),
        scratch_shapes=[
            pltpu.VMEM((PEERS_COL * 128, 128), F32),
            pltpu.VMEM((8 * COLS, EMB), BF16),
            pltpu.VMEM((256, 128 * STEP), BF16),
            pltpu.VMEM((PART * COLS, 1024), BF16),
            pltpu.VMEM((PART * COLS, 1024), BF16),
        ],
        compiler_params=params(63),
        name="outer_update",
    )(left, right, w, offset, keep_i, keep_j, z)


def tables():
    expand = np.zeros((128, 4, 4, HEAD), np.float32)
    for u in range(4):
        for d in range(HEAD):
            expand[u * HEAD + d, u, :, d] = 1
    perm = np.zeros((ROWS, ROWS), np.float32)
    for i in range(ROWS):
        half, rest = divmod(i, HALF)
        perm[half * HALF + (rest % 4) * QUADS + rest // 4, i] = 1
    return expand.reshape(128, 512), perm


def swap_cores(x):
    return lax.ppermute(x, "core", [(0, 1), (1, 0)])


def along_y(x, d):
    return lax.ppermute(x, "y", [(a, (a + d) % 4) for a in range(4)])


def turn_grid(x):
    def index(a, b, c, d):
        return ((a * 2 + b) * 4 + c) * 2 + d

    moves = [
        (index(a, b, c, d), index(c, d, a, b)) for a in range(4) for b in range(2) for c in range(4) for d in range(2)
    ]
    return lax.ppermute(x, ("x", "zl", "y", "zh"), moves)


def on_device(
    alignment_embedding,
    couplings_embedding,
    alignment_availability,
    amino_availability,
    alignment_scaling_vector,
    attention_joint_matrix,
    attention_final_matrix,
    coupling_scaling_vector,
    coupling_logit_matrix,
    tensor_scaling_vector,
    first_factor_matrix,
    second_factor_matrix,
    tensor_projection_matrix,
    tensor_offset_vector,
):
    core = lax.axis_index("core")
    at = jnp.stack([lax.axis_index(name) for name in ("y", "core")]).astype(jnp.int32)
    expand, perm = tables()

    bias = pair_bias(
        couplings_embedding.reshape(ROWS * COLS, PAIR),
        coupling_scaling_vector[None],
        coupling_logit_matrix.T,
    ).reshape(4 * HEADS, QUADS, 4 * COLS)
    bias = lax.all_to_all(bias, ROW + ("zh", "core"), 0, 0, tiled=True).reshape(8, 4, QUADS, 4 * COLS)

    keep = amino_availability.astype(F32)
    keep_i = lax.dynamic_slice_in_dim(keep, lax.axis_index(ROW) * ROWS, ROWS)
    keep_j = lax.dynamic_slice_in_dim(keep, lax.axis_index(COL) * COLS, COLS)
    keep_j = jnp.pad(keep_j, (0, 128 - COLS))[None]
    present = alignment_availability.astype(BF16)
    sent_mask = jnp.pad(
        jnp.stack([present[:, :128], jnp.pad(present[:, 128:], ((0, 0), (0, 64)))]), ((0, 0), (0, 4), (0, 0))
    ).reshape(16, 128)
    own, gate, keep_j = project(
        alignment_embedding,
        alignment_scaling_vector[None],
        attention_joint_matrix,
        jnp.asarray(expand, BF16),
        jnp.asarray(perm, BF16),
        sent_mask,
        keep_j,
    )
    own, bias, at, keep_i = lax.optimization_barrier((own, bias, at, keep_i))
    up, down = along_y(bias, 1), along_y(bias, 3)
    own = lax.all_to_all(own, ROW, 0, 0, tiled=True)
    own = lax.optimization_barrier((own, up, down))[0]
    pieces = (bias, up, down, along_y(up[:, :2], 1), along_y(down[:, 2:], 3))
    k, v, q = prepare(at, own, swap_cores(own))
    attended = attend(at, k, v, q, pieces).reshape(16, HALF, 128)
    attended = lax.all_to_all(attended, ROW + ("core",), 0, 0, tiled=True).reshape(HEADS, ROWS, 128)

    present = alignment_availability.astype(F32)
    alignment_refreshed, left, right = finish(
        attended,
        gate,
        alignment_embedding,
        attention_final_matrix,
        jnp.asarray(perm.T, BF16),
        tensor_scaling_vector[None],
        jnp.tile(first_factor_matrix, (1, 4)),
        jnp.tile(second_factor_matrix, (1, 4)),
        jnp.repeat(present.T, HEAD, axis=1),
    )
    left = lax.all_to_all(left, ("y", "zh"), 0, 0, tiled=True)
    right = jnp.broadcast_to(turn_grid(right)[None], (8, ROWS, 128)).reshape(PEERS_COL, COLS, 128)
    right = lax.all_to_all(right, ROW + ("core",), 0, 0, tiled=True)

    projection = (tensor_projection_matrix.astype(F32) / 64).astype(BF16)
    projection = projection.reshape(HEAD, 8, 4, PAIR).transpose(1, 2, 0, 3).reshape(1024, PAIR)
    couplings_refreshed = outer_update(
        lines(at, left, swap_cores(left)),
        right,
        projection,
        tensor_offset_vector[None],
        keep_i,
        keep_j,
        couplings_embedding,
    )
    return alignment_refreshed, couplings_refreshed


def solution(mesh):
    mesh = Mesh(mesh.devices.reshape(4, 2, 4, 2, 2), ROW + COL)
    placed = (P(COL, ROW, None), P(ROW, COL, None), P(COL, ROW)) + (P(),) * 11
    return jax.shard_map(
        on_device,
        mesh=mesh,
        in_specs=placed,
        out_specs=(P(COL, ROW, None), P(ROW, COL, None)),
        check_vma=False,
    )
```
